128 devices in a mesh: layer: 16 (over y, z_lo, core), tile: 8 (over x, z_hi).
Axes of the slice: x: 4, y: 4, z: 4 (z_hi: 2, z_lo: 2; z = z_hi * 2 + z_lo), core: 2. Of those that a mesh axis runs over, the one named last changes fastest.
Arguments:
- incident: bfloat16 [4096, 128], P('tile'), may hold values from -6 to 6
- interface: bfloat16 [32, 4096, 4096], P('layer', 'tile'), may hold values from -0.09375 to 0.09375
- eigvec: bfloat16 [32, 4096, 4096], P('layer', 'tile'), may hold values from -0.09375 to 0.09375
- angle: float32 [32, 4096], P('layer'), may hold values from -3.140625 to 3.140625
- decay: float32 [32, 4096], P('layer'), may hold values from 0.002 to 0.15
Outputs:
- fields: bfloat16 [32, 4096, 512], P('layer', 'tile')
- leaving: float32 [32, 4096, 128], P('layer', 'tile')
The draws below stay inside these ranges and needn't reach their ends.
All inputs are finite; a program needn't handle non-finite values.
Results may differ from the reference program's by a relative error of at most 0.035.
Values sent between devices are 32-bit elements; how exact they have to be, the bound alone decides.
No kernel may reach another device: no remote copies, remote signals or barrier semaphores. Data moves between devices by JAX's collectives and lax.ppermute only.
A program may use at most 128 MiB of HBM per device.

```python
import math
import jax
import jax.numpy as jnp
from jax import lax

M = 4096
COLS = 64
DEPTHS = 4
LAYERS = 32


def steps_of(stream_key, extent, shards, least, top_value):
    def one(position, parts):
        heights = jax.random.uniform(jax.random.fold_in(jax.random.fold_in(stream_key, 6), position), (parts,), jnp.float32, least / len(shards), top_value / len(shards))
        return jnp.repeat(jnp.exp(heights), extent[position] // parts).reshape((-1,) + (1,) * (len(extent) - position - 1))

    factor_of = one(*shards[0])
    for cut in shards[1:]:
        factor_of = factor_of * one(*cut)
    return factor_of


def centred(own_key, dims, scale, limit, shards=(), held_as=jnp.bfloat16):
    gain = steps_of(own_key, dims, shards, -0.22, 0.18) if shards else 1.0
    entries = jax.random.normal(own_key, dims, jnp.float32) * scale * gain
    return jnp.minimum(jnp.maximum(entries, -limit), limit).astype(held_as)


def setup_inputs(seed: int = 0) -> dict:
    seeds = jax.random.split(jax.random.key(seed), 6)
    return {
        "incident": centred(seeds[0], (M, 2 * COLS), 1.0, 6.0, ((0, 8),)),
        "interface": centred(seeds[1], (LAYERS, M, M), ((M * 19) // 20) ** -0.5, 0.09375, ((0, 16), (1, 8))),
        "eigvec": centred(seeds[2], (LAYERS, M, M), M ** -0.5, 0.09375, ((0, 16), (1, 8))),
        "angle": jnp.clip(jax.random.uniform(seeds[3], (LAYERS, M), jnp.float32, -3.140625, 3.140625), -3.140625, 3.140625),
        "decay": jnp.clip(jnp.exp(math.log(0.15) - 4.317488 * jax.random.uniform(seeds[4], (LAYERS, M), jnp.float32) ** steps_of(seeds[4], (LAYERS, M), ((0, 16),), -0.2, 0.2)), 0.002, 0.15),
    }


def rotate(block, angle_row, decay_row, frac):
    values = block.astype(jnp.float32)
    half = values.shape[1] // 2
    real_part = values[:, :half]
    imag_part = values[:, half:]
    scale = jnp.exp(-frac * decay_row)
    cosine = (scale * jnp.cos(frac * angle_row))[:, None]
    sine = (scale * jnp.sin(frac * angle_row))[:, None]
    return jnp.concatenate([cosine * real_part - sine * imag_part, sine * real_part + cosine * imag_part], axis=1)


def reference(incident, interface, eigvec, angle, decay):
    def one_layer(enter, items):
        s_mat, w_mat, angle_row, decay_row = items
        phased = rotate(enter, angle_row, decay_row, 1.0).astype(jnp.bfloat16)
        leave = jnp.dot(s_mat, phased, preferred_element_type=jnp.float32)
        depth = jnp.concatenate([rotate(enter, angle_row, decay_row, step / DEPTHS).astype(jnp.bfloat16) for step in range(DEPTHS)], axis=1)
        field = jnp.dot(w_mat, depth, preferred_element_type=jnp.float32).astype(jnp.bfloat16)
        return leave, (field, leave)

    final, outputs = lax.scan(one_layer, incident.astype(jnp.float32), (interface, eigvec, angle, decay))
    return outputs[0], outputs[1]
```

```python
import functools

import jax
import jax.numpy as jnp
from jax import lax
from jax.experimental import pallas as pl
from jax.experimental.pallas import tpu as pltpu
from jax.sharding import PartitionSpec as P

DEPTHS = 4
CHUNKS = 4
NT = (((1,), (1,)), ((), ()))


def step_kernel(full_ref, cos_ref, sin_ref, mat_ref, out_ref, mat_buf, sems, *, layer):
    blocks, wide, rows = full_ref.shape
    half = wide // 2
    copies = [
        pltpu.make_async_copy(
            mat_ref.at[layer, :, pl.ds(b * rows, rows)], mat_buf.at[b], sems.at[b]
        )
        for b in range(blocks)
    ]
    for copy in copies:
        copy.start()
    total = jnp.zeros((wide, rows), jnp.float32)
    for b in range(blocks):
        cosine = cos_ref[b : b + 1, :]
        sine = sin_ref[b : b + 1, :]
        real_part = full_ref[b, :half, :]
        imag_part = full_ref[b, half:, :]
        phased = jnp.concatenate(
            [cosine * real_part - sine * imag_part, sine * real_part + cosine * imag_part], axis=0
        ).astype(jnp.bfloat16)
        copies[b].wait()
        total += lax.dot_general(phased, mat_buf[b], NT, preferred_element_type=jnp.float32)
    for b in range(blocks):
        out_ref[b] = total


def layer_step(full, cosine, sine, mats, layer):
    blocks, wide, rows = full.shape
    vmem = pl.BlockSpec(memory_space=pltpu.VMEM)
    return pl.pallas_call(
        functools.partial(step_kernel, layer=layer),
        out_shape=jax.ShapeDtypeStruct(full.shape, jnp.float32),
        in_specs=[vmem, vmem, vmem, pl.BlockSpec(memory_space=pl.ANY)],
        out_specs=vmem,
        scratch_shapes=[
            pltpu.VMEM((blocks, rows, rows), jnp.bfloat16),
            pltpu.SemaphoreType.DMA((blocks,)),
        ],
        compiler_params=pltpu.CompilerParams(vmem_limit_bytes=24 * 1024 * 1024),
    )(full, cosine, sine, mats)


def fields_kernel(enter_ref, cos_ref, sin_ref, mat_ref, out_ref, total):
    step = pl.program_id(1)
    chunks, _, wide, rows = enter_ref.shape[1:]
    half = wide // 2
    real_part = enter_ref[0, :, 0, :half, :].reshape(chunks * half, rows)
    imag_part = enter_ref[0, :, 0, half:, :].reshape(chunks * half, rows)
    parts = [real_part.astype(jnp.bfloat16), imag_part.astype(jnp.bfloat16)]
    for depth in range(1, DEPTHS):
        cosine = cos_ref[0, 0, depth - 1 : depth, :]
        sine = sin_ref[0, 0, depth - 1 : depth, :]
        parts.append((cosine * real_part - sine * imag_part).astype(jnp.bfloat16))
        parts.append((sine * real_part + cosine * imag_part).astype(jnp.bfloat16))
    depths = jnp.concatenate(parts, axis=0)
    partial = lax.dot_general(mat_ref[0], depths, NT, preferred_element_type=jnp.float32)

    @pl.when(step == 0)
    def _():
        total[...] = partial

    @pl.when(step > 0)
    def _():
        total[...] += partial

    @pl.when(step == pl.num_programs(1) - 1)
    def _():
        out_ref[0] = total[...].astype(jnp.bfloat16)


def all_fields(enters, cosines, sines, eigvec):
    layers, chunks, blocks, wide, rows = enters.shape
    orders = eigvec.shape[2]
    cols = DEPTHS * chunks * wide
    coef = pl.BlockSpec((1, 1, DEPTHS - 1, rows), lambda i, b: (i, b, 0, 0))
    return pl.pallas_call(
        fields_kernel,
        out_shape=jax.ShapeDtypeStruct((layers, rows, cols), jnp.bfloat16),
        grid=(layers, blocks),
        in_specs=[
            pl.BlockSpec((1, chunks, 1, wide, rows), lambda i, b: (i, 0, b, 0, 0)),
            coef,
            coef,
            pl.BlockSpec((1, rows, rows), lambda i, b: (i, 0, b)),
        ],
        out_specs=pl.BlockSpec((1, rows, cols), lambda i, b: (i, 0, 0)),
        scratch_shapes=[pltpu.VMEM((rows, cols), jnp.float32)],
        compiler_params=pltpu.CompilerParams(vmem_limit_bytes=32 * 1024 * 1024),
    )(enters, cosines, sines, eigvec)


def to_all(block):
    return lax.all_to_all(block, "tile", split_axis=0, concat_axis=0, tiled=False)


def on_device(incident, interface, eigvec, angle, decay):
    groups = lax.axis_size("layer")
    tiles = lax.axis_size("tile")
    member = lax.axis_index("layer")
    layers, rows, orders = interface.shape
    width = incident.shape[1]
    half = width // 2
    part = half // CHUNKS
    wide = 2 * part

    angle = angle.reshape(layers, tiles, 1, rows)
    decay = decay.reshape(layers, tiles, 1, rows)
    fracs = (jnp.arange(1, DEPTHS + 1, dtype=jnp.float32) / DEPTHS).reshape(1, 1, DEPTHS, 1)
    scale = jnp.exp(-fracs * decay)
    cosines = scale * jnp.cos(fracs * angle)
    sines = scale * jnp.sin(fracs * angle)
    whole_cos, whole_sin = cosines[:, :, DEPTHS - 1], sines[:, :, DEPTHS - 1]

    start = incident.astype(jnp.float32).T.reshape(2, CHUNKS, part, rows)
    start = start.transpose(1, 0, 2, 3).reshape(CHUNKS, wide, rows)

    ring = [(i, (i + 1) % groups) for i in range(groups)]
    enters = jnp.zeros((layers, CHUNKS + 1, tiles, wide, rows), jnp.float32)
    leaves = jnp.zeros((layers, CHUNKS + 1, wide, rows), jnp.float32)
    received = None
    for tick in range(groups + CHUNKS - 1):
        own = start[min(tick, CHUNKS - 1)]
        inbox = own if received is None else jnp.where(member == 0, own, received)
        slot = jnp.clip(tick - member, 0, CHUNKS)
        spread = jnp.broadcast_to(inbox[None], (tiles, wide, rows))
        for layer in range(layers):
            full = to_all(spread)
            spread = layer_step(full, whole_cos[layer], whole_sin[layer], interface, layer)
            enters = lax.dynamic_update_slice(enters, full[None, None], (layer, slot, 0, 0, 0))
            leaves = lax.dynamic_update_slice(leaves, spread[:1][None], (layer, slot, 0, 0))
        received = lax.ppermute(spread[0], "layer", ring)

    fields = all_fields(
        enters[:, :CHUNKS], cosines[:, :, : DEPTHS - 1], sines[:, :, : DEPTHS - 1], eigvec
    )
    leaving = leaves[:, :CHUNKS].reshape(layers, CHUNKS, 2, part, rows)
    leaving = leaving.transpose(0, 4, 2, 1, 3).reshape(layers, rows, width)
    return fields, leaving


def solution(mesh):
    in_specs = (
        P("tile", None),
        P("layer", "tile", None),
        P("layer", "tile", None),
        P("layer", None),
        P("layer", None),
    )
    out_specs = (P("layer", "tile", None), P("layer", "tile", None))
    return jax.shard_map(
        on_device, mesh=mesh, in_specs=in_specs, out_specs=out_specs, check_vma=False
    )
```

```python
import functools

import jax
import jax.numpy as jnp
from jax import lax
from jax.experimental import pallas as pl
from jax.experimental.pallas import tpu as pltpu
from jax.sharding import PartitionSpec as P

DEPTHS = 4
CHUNKS = 2
CORES = 2
PIECES = 8
NT = (((1,), (1,)), ((), ()))
VMEM = pl.BlockSpec(memory_space=pltpu.VMEM)
VMEM_LIMIT = 58 * 1024 * 1024


def load_kernel(core_ref, own_ref, other_ref, out_ref):
    core = core_ref[0]
    own = own_ref[0]
    other = other_ref[...].astype(jnp.bfloat16)
    out_ref[0] = jnp.where(core == 0, own, other)
    out_ref[1] = jnp.where(core == 0, other, own)


def load_pair(core, own, other, layer):
    rows, orders = other.shape
    piece = rows // PIECES
    return pl.pallas_call(
        load_kernel,
        out_shape=jax.ShapeDtypeStruct((CORES, rows, orders), jnp.bfloat16),
        grid=(PIECES,),
        in_specs=[
            pl.BlockSpec(memory_space=pltpu.SMEM),
            pl.BlockSpec((1, piece, orders), lambda p: (layer, p, 0)),
            pl.BlockSpec((piece, orders), lambda p: (p, 0)),
        ],
        out_specs=pl.BlockSpec((CORES, piece, orders), lambda p: (0, p, 0)),
        compiler_params=pltpu.CompilerParams(vmem_limit_bytes=VMEM_LIMIT),
    )(core, own, other)


def step_kernel(full_ref, phase_ref, mat_ref, out_ref, phase_buf, mat_buf, phase_sem, sems, *, half, layer):
    blocks, wide, rows = full_ref.shape
    split = wide // 2
    phase_copy = pltpu.make_async_copy(phase_ref.at[layer], phase_buf, phase_sem)
    phase_copy.start()
    copies = [
        pltpu.make_async_copy(
            mat_ref.at[half, :, pl.ds(b * rows, rows)], mat_buf.at[b], sems.at[b]
        )
        for b in range(blocks)
    ]
    for copy in copies:
        copy.start()
    total = jnp.zeros((wide, rows), jnp.float32)
    phase_copy.wait()
    for b in range(blocks):
        cosine = phase_buf[0, b : b + 1, :]
        sine = phase_buf[1, b : b + 1, :]
        real_part = full_ref[b, :split, :]
        imag_part = full_ref[b, split:, :]
        phased = jnp.concatenate(
            [cosine * real_part - sine * imag_part, sine * real_part + cosine * imag_part], axis=0
        ).astype(jnp.bfloat16)
        copies[b].wait()
        total += lax.dot_general(phased, mat_buf[b], NT, preferred_element_type=jnp.float32)
    for b in range(blocks):
        out_ref[b] = total


def layer_step(full, phases, pair, half, layer):
    blocks, wide, rows = full.shape
    anywhere = pl.BlockSpec(memory_space=pl.ANY)
    return pl.pallas_call(
        functools.partial(step_kernel, half=half, layer=layer),
        out_shape=jax.ShapeDtypeStruct(full.shape, jnp.float32),
        in_specs=[VMEM, anywhere, anywhere],
        out_specs=VMEM,
        scratch_shapes=[
            pltpu.VMEM((2, blocks, rows), jnp.float32),
            pltpu.VMEM((blocks, rows, rows), jnp.bfloat16),
            pltpu.SemaphoreType.DMA,
            pltpu.SemaphoreType.DMA((blocks,)),
        ],
        compiler_params=pltpu.CompilerParams(vmem_limit_bytes=VMEM_LIMIT),
    )(full, phases, pair)


def fields_kernel(core_ref, own_ref, other_ref, cos_ref, sin_ref, mat_ref, out_ref, total):
    step = pl.program_id(0)
    chunks, wide, rows = own_ref.shape[1], own_ref.shape[3], own_ref.shape[4]
    half = wide // 2
    first = core_ref[0] == 0

    def columns(part):
        own = own_ref[0, :, 0, part, :].reshape(chunks * half, rows)
        other = other_ref[0, :, 0, part, :].reshape(chunks * half, rows)
        low = jnp.where(first, own, other)
        high = jnp.where(first, other, own)
        return jnp.concatenate([low, high], axis=0)

    real_part = columns(slice(0, half))
    imag_part = columns(slice(half, wide))
    parts = [real_part.astype(jnp.bfloat16), imag_part.astype(jnp.bfloat16)]
    for depth in range(DEPTHS - 1):
        cosine = cos_ref[0, depth : depth + 1, :]
        sine = sin_ref[0, depth : depth + 1, :]
        parts.append((cosine * real_part - sine * imag_part).astype(jnp.bfloat16))
        parts.append((sine * real_part + cosine * imag_part).astype(jnp.bfloat16))
    depths = jnp.concatenate(parts, axis=0)
    partial = lax.dot_general(mat_ref[0], depths, NT, preferred_element_type=jnp.float32)

    @pl.when(step == 0)
    def _():
        total[...] = partial

    @pl.when(step > 0)
    def _():
        total[...] += partial

    @pl.when(step == pl.num_programs(0) - 1)
    def _():
        out_ref[...] = total[...].astype(jnp.bfloat16)


def layer_fields(core, own, other, cosines, sines, eigvec, layer):
    chunks = other.shape[1]
    wide, rows = other.shape[3], other.shape[4]
    blocks = eigvec.shape[2] // rows
    cols = DEPTHS * CORES * chunks * wide
    coef = pl.BlockSpec((1, DEPTHS, rows), lambda b, c: (b, 0, 0))
    return pl.pallas_call(
        fields_kernel,
        out_shape=jax.ShapeDtypeStruct((rows, cols), jnp.bfloat16),
        grid_spec=pltpu.PrefetchScalarGridSpec(
            num_scalar_prefetch=1,
            grid=(blocks,),
            in_specs=[
                pl.BlockSpec((1, chunks, 1, wide, rows), lambda b, c: (c[0], 0, b, 0, 0)),
                pl.BlockSpec((1, chunks, 1, wide, rows), lambda b, c: (0, 0, b, 0, 0)),
                coef,
                coef,
                pl.BlockSpec((1, rows, rows), lambda b, c: (layer, 0, b)),
            ],
            out_specs=pl.BlockSpec((rows, cols), lambda b, c: (0, 0)),
            scratch_shapes=[pltpu.VMEM((rows, cols), jnp.float32)],
        ),
        compiler_params=pltpu.CompilerParams(vmem_limit_bytes=VMEM_LIMIT),
    )(core, own, other, cosines, sines, eigvec)


def to_all(block):
    return lax.all_to_all(block, "tile", split_axis=0, concat_axis=0, tiled=False)


def on_device(incident, interface, eigvec, angle, decay):
    groups = lax.axis_size("layer")
    tiles = lax.axis_size("tile")
    member = lax.axis_index("layer")
    core = member % CORES
    stage = member // CORES
    stages = groups // CORES
    layers, rows, orders = interface.shape
    width = incident.shape[1]
    part = width // 2 // CORES // CHUNKS
    wide = 2 * part
    core_arg = core.astype(jnp.int32).reshape(1)
    partner = [(i, i ^ 1) for i in range(groups)]
    ring = [(i, (i + CORES) % groups) for i in range(groups)]

    phases = jnp.stack([angle, decay]).reshape(2, layers, tiles, rows)
    other_phases = lax.ppermute(phases, "layer", partner)
    mats = []
    for layer in range(layers):
        other = lax.ppermute(interface[layer].astype(jnp.float32), "layer", partner)
        mats.append(load_pair(core_arg, interface, other, layer))
    early = jnp.where(core == 0, phases, other_phases)
    late = jnp.where(core == 0, other_phases, phases)
    all_phases = jnp.concatenate([early, late], axis=1)
    scale = jnp.exp(-all_phases[1])
    whole = jnp.stack([scale * jnp.cos(all_phases[0]), scale * jnp.sin(all_phases[0])], axis=1)
    fracs = (jnp.arange(1, DEPTHS + 1, dtype=jnp.float32) / DEPTHS).reshape(1, 1, DEPTHS, 1)
    scale = jnp.exp(-fracs * phases[1][:, :, None, :])
    cosines = scale * jnp.cos(fracs * phases[0][:, :, None, :])
    sines = scale * jnp.sin(fracs * phases[0][:, :, None, :])

    start = incident.astype(jnp.float32).T.reshape(2, CORES, CHUNKS, part, rows)
    start = jnp.where(core == 0, start[:, 0], start[:, 1])
    start = start.transpose(1, 0, 2, 3).reshape(CHUNKS, wide, rows)

    saved = [
        jnp.zeros((CORES, CHUNKS + 1, tiles + 1, wide, rows), jnp.float32) for _ in range(layers)
    ]
    received = None
    for tick in range(stages + CHUNKS - 1):
        inbox = start[min(tick, CHUNKS - 1)]
        if tick > 0:
            inbox = jnp.where(stage == 0, inbox, received)
        slot = tick - stage
        slot = jnp.where((slot >= 0) & (slot < CHUNKS), slot, CHUNKS)
        spread = jnp.broadcast_to(inbox[None], (tiles, wide, rows))
        for layer in range(CORES * layers):
            full = to_all(spread)
            own, half = layer % layers, layer // layers
            spread = layer_step(full, whole, mats[own], half, layer)
            place = (half, slot, 0, 0, 0)
            saved[own] = lax.dynamic_update_slice(saved[own], full[None, None], place)
            place = (half, slot, tiles, 0, 0)
            saved[own] = lax.dynamic_update_slice(saved[own], spread[None, None, :1], place)
        received = lax.ppermute(spread[0], "layer", ring)

    fields = []
    leaving = []
    for layer in range(layers):
        shape = (1, CHUNKS, tiles + 1, wide, rows)
        send = lax.dynamic_slice(saved[layer], (1 - core, 0, 0, 0, 0), shape)
        other = lax.ppermute(send, "layer", partner)
        fields.append(
            layer_fields(
                core_arg, saved[layer], other, cosines[layer], sines[layer], eigvec, layer
            )
        )
        shape = (1, CHUNKS, 1, wide, rows)
        own_leave = lax.dynamic_slice(saved[layer], (core, 0, tiles, 0, 0), shape)
        other_leave = other[:, :, tiles:]
        leave = jnp.concatenate(
            [
                jnp.where(core == 0, own_leave, other_leave),
                jnp.where(core == 0, other_leave, own_leave),
            ]
        ).reshape(CORES, CHUNKS, 2, part, rows)
        leaving.append(leave.transpose(4, 2, 0, 1, 3).reshape(rows, width))
    return jnp.stack(fields), jnp.stack(leaving)


def solution(mesh):
    in_specs = (
        P("tile", None),
        P("layer", "tile", None),
        P("layer", "tile", None),
        P("layer", None),
        P("layer", None),
    )
    out_specs = (P("layer", "tile", None), P("layer", "tile", None))
    return jax.shard_map(
        on_device, mesh=mesh, in_specs=in_specs, out_specs=out_specs, check_vma=False
    )
```

```python
import functools

import jax
import jax.numpy as jnp
from jax import lax
from jax.experimental import pallas as pl
from jax.experimental.pallas import tpu as pltpu
from jax.sharding import PartitionSpec as P

DEPTHS = 4
CHUNKS = 2
CORES = 2
PIECES = 8
NT = (((1,), (1,)), ((), ()))
VMEM = pl.BlockSpec(memory_space=pltpu.VMEM)
ANYWHERE = pl.BlockSpec(memory_space=pl.ANY)
VMEM_LIMIT = 48 * 1024 * 1024


def widen_kernel(mat_ref, after_ref, out_ref):
    out_ref[...] = mat_ref[0].astype(jnp.float32)


def widen(mats, layer, after):
    rows, orders = mats.shape[1:]
    piece = rows // PIECES
    return pl.pallas_call(
        widen_kernel,
        out_shape=jax.ShapeDtypeStruct((rows, orders), jnp.float32),
        grid=(PIECES,),
        in_specs=[pl.BlockSpec((1, piece, orders), lambda p: (layer, p, 0)), ANYWHERE],
        out_specs=pl.BlockSpec((piece, orders), lambda p: (p, 0)),
        compiler_params=pltpu.CompilerParams(vmem_limit_bytes=VMEM_LIMIT),
    )(mats, after)


def narrow_kernel(mat_ref, *refs):
    refs[-1][0] = mat_ref[...].astype(jnp.bfloat16)


def narrow(mat, layer, layers, before):
    rows, orders = mat.shape
    piece = rows // PIECES
    return pl.pallas_call(
        narrow_kernel,
        out_shape=jax.ShapeDtypeStruct((layers, rows, orders), jnp.bfloat16),
        grid=(PIECES,),
        in_specs=[pl.BlockSpec((piece, orders), lambda p: (p, 0))] + [ANYWHERE] * len(before),
        out_specs=pl.BlockSpec((1, piece, orders), lambda p: (layer, p, 0)),
        input_output_aliases={1: 0} if before else {},
        compiler_params=pltpu.CompilerParams(vmem_limit_bytes=VMEM_LIMIT),
    )(mat, *before)


def step_kernel(
    core_ref, full_ref, phase_ref, own_ref, other_ref, out_ref, row_buf, mat_buf, row_sem, sems,
    *, half, layer, number
):
    blocks, wide, rows = full_ref.shape
    split = wide // 2
    row_copy = pltpu.make_async_copy(phase_ref.at[number], row_buf, row_sem)
    row_copy.start()

    def copies(mats_ref):
        return [
            pltpu.make_async_copy(
                mats_ref.at[layer, :, pl.ds(b * rows, rows)], mat_buf.at[b], sems.at[b]
            )
            for b in range(blocks)
        ]

    @pl.when(core_ref[0] == half)
    def _():
        for copy in copies(own_ref):
            copy.start()

    @pl.when(core_ref[0] != half)
    def _():
        for copy in copies(other_ref):
            copy.start()

    arrivals = copies(own_ref)
    total = jnp.zeros((wide, rows), jnp.float32)
    row_copy.wait()
    for b in range(blocks):
        cosine = row_buf[0, b : b + 1, :]
        sine = row_buf[1, b : b + 1, :]
        real_part = full_ref[b, :split, :]
        imag_part = full_ref[b, split:, :]
        phased = jnp.concatenate(
            [cosine * real_part - sine * imag_part, sine * real_part + cosine * imag_part], axis=0
        ).astype(jnp.bfloat16)
        arrivals[b].wait()
        total += lax.dot_general(phased, mat_buf[b], NT, preferred_element_type=jnp.float32)
    for b in range(blocks):
        out_ref[b] = total


def layer_step(core, full, phases, own, other, half, layer, number):
    blocks, wide, rows = full.shape
    return pl.pallas_call(
        functools.partial(step_kernel, half=half, layer=layer, number=number),
        out_shape=jax.ShapeDtypeStruct(full.shape, jnp.float32),
        in_specs=[pl.BlockSpec(memory_space=pltpu.SMEM), VMEM] + [ANYWHERE] * 3,
        out_specs=VMEM,
        scratch_shapes=[
            pltpu.VMEM(phases.shape[1:], jnp.float32),
            pltpu.VMEM((blocks, rows, rows), jnp.bfloat16),
            pltpu.SemaphoreType.DMA,
            pltpu.SemaphoreType.DMA((blocks,)),
        ],
        compiler_params=pltpu.CompilerParams(vmem_limit_bytes=VMEM_LIMIT),
        cost_estimate=pl.CostEstimate(
            flops=2 * wide * rows * rows * blocks,
            bytes_accessed=2 * blocks * rows * rows,
            transcendentals=0,
        ),
    )(core, full, phases, own, other)


def fields_kernel(core_ref, own_ref, other_ref, cos_ref, sin_ref, mat_ref, *refs):
    out_ref, total = refs[-2:]
    step = pl.program_id(0)
    chunks, wide, rows = own_ref.shape[1], own_ref.shape[3], own_ref.shape[4]
    half = wide // 2
    first = core_ref[0] == 0

    def columns(part):
        own = own_ref[0, :, 0, part, :].reshape(chunks * half, rows)
        other = other_ref[0, :, 0, part, :].reshape(chunks * half, rows)
        low = jnp.where(first, own, other)
        high = jnp.where(first, other, own)
        return jnp.concatenate([low, high], axis=0)

    real_part = columns(slice(0, half))
    imag_part = columns(slice(half, wide))
    parts = [real_part.astype(jnp.bfloat16), imag_part.astype(jnp.bfloat16)]
    for depth in range(DEPTHS - 1):
        cosine = cos_ref[0, depth : depth + 1, :]
        sine = sin_ref[0, depth : depth + 1, :]
        parts.append((cosine * real_part - sine * imag_part).astype(jnp.bfloat16))
        parts.append((sine * real_part + cosine * imag_part).astype(jnp.bfloat16))
    depths = jnp.concatenate(parts, axis=0)
    partial = lax.dot_general(mat_ref[0], depths, NT, preferred_element_type=jnp.float32)

    @pl.when(step == 0)
    def _():
        total[...] = partial

    @pl.when(step > 0)
    def _():
        total[...] += partial

    @pl.when(step == pl.num_programs(0) - 1)
    def _():
        out_ref[0] = total[...].astype(jnp.bfloat16)


def layer_fields(core, own, other, cosines, sines, eigvec, layer, before):
    chunks = other.shape[1]
    wide, rows = other.shape[3], other.shape[4]
    blocks = eigvec.shape[2] // rows
    cols = DEPTHS * CORES * chunks * wide
    coef = pl.BlockSpec((1, DEPTHS, rows), lambda b, c: (b, 0, 0))
    return pl.pallas_call(
        fields_kernel,
        out_shape=jax.ShapeDtypeStruct((eigvec.shape[0], rows, cols), jnp.bfloat16),
        grid_spec=pltpu.PrefetchScalarGridSpec(
            num_scalar_prefetch=1,
            grid=(blocks,),
            in_specs=[
                pl.BlockSpec((1, chunks, 1, wide, rows), lambda b, c: (c[0], 0, b, 0, 0)),
                pl.BlockSpec((1, chunks, 1, wide, rows), lambda b, c: (0, 0, b, 0, 0)),
                coef,
                coef,
                pl.BlockSpec((1, rows, rows), lambda b, c: (layer, 0, b)),
            ]
            + [ANYWHERE] * len(before),
            out_specs=pl.BlockSpec((1, rows, cols), lambda b, c: (layer, 0, 0)),
            scratch_shapes=[pltpu.VMEM((rows, cols), jnp.float32)],
        ),
        input_output_aliases={6: 0} if before else {},
        compiler_params=pltpu.CompilerParams(vmem_limit_bytes=VMEM_LIMIT),
    )(core, own, other, cosines, sines, eigvec, *before)


def to_all(block):
    return lax.all_to_all(block, "tile", split_axis=0, concat_axis=0, tiled=False)


def on_device(incident, interface, eigvec, angle, decay):
    groups = lax.axis_size("layer")
    tiles = lax.axis_size("tile")
    member = lax.axis_index("layer")
    core = member % CORES
    stage = member // CORES
    stages = groups // CORES
    layers, rows, orders = interface.shape
    width = incident.shape[1]
    part = width // 2 // CORES // CHUNKS
    wide = 2 * part
    core_arg = core.astype(jnp.int32).reshape(1)
    partner = [(i, i ^ 1) for i in range(groups)]
    ring = [(i, (i + CORES) % groups) for i in range(groups)]

    phases = jnp.stack([angle, decay]).reshape(2, layers, tiles, rows)
    other_phases = lax.ppermute(phases, "layer", partner)
    wide_mats = []
    arrived = []
    for layer in range(layers):
        wide_mats.append(widen(interface, layer, wide_mats[-1] if layer else incident))
        arrived.append(lax.ppermute(wide_mats[layer], "layer", partner))
    others = ()
    early = jnp.where(core == 0, phases, other_phases)
    late = jnp.where(core == 0, other_phases, phases)
    all_phases = jnp.concatenate([early, late], axis=1)
    scale = jnp.exp(-all_phases[1])
    whole = jnp.stack([scale * jnp.cos(all_phases[0]), scale * jnp.sin(all_phases[0])], axis=1)
    fracs = (jnp.arange(1, DEPTHS + 1, dtype=jnp.float32) / DEPTHS).reshape(1, 1, DEPTHS, 1)
    scale = jnp.exp(-fracs * phases[1][:, :, None, :])
    cosines = scale * jnp.cos(fracs * phases[0][:, :, None, :])
    sines = scale * jnp.sin(fracs * phases[0][:, :, None, :])

    start = incident.astype(jnp.float32).T.reshape(2, CORES, CHUNKS, part, rows)
    start = jnp.where(core == 0, start[:, 0], start[:, 1])
    start = start.transpose(1, 0, 2, 3).reshape(CHUNKS, wide, rows)

    saved = [
        jnp.zeros((CORES, CHUNKS + 1, tiles + 1, wide, rows), jnp.float32) for _ in range(layers)
    ]
    fields = []
    leaving = []

    def finish(layer):
        shape = (1, CHUNKS, tiles + 1, wide, rows)
        send = lax.dynamic_slice(saved[layer], (1 - core, 0, 0, 0, 0), shape)
        other = lax.ppermute(send, "layer", partner)
        fields[:] = [
            layer_fields(
                core_arg, saved[layer], other, cosines[layer], sines[layer], eigvec, layer, fields
            )
        ]
        shape = (1, CHUNKS, 1, wide, rows)
        own_leave = lax.dynamic_slice(saved[layer], (core, 0, tiles, 0, 0), shape)
        other_leave = other[:, :, tiles:]
        leave = jnp.concatenate(
            [
                jnp.where(core == 0, own_leave, other_leave),
                jnp.where(core == 0, other_leave, own_leave),
            ]
        ).reshape(CORES, CHUNKS, 2, part, rows)
        leaving.append(leave.transpose(4, 2, 0, 1, 3).reshape(rows, width))

    received = None
    for tick in range(stages + CHUNKS - 1):
        inbox = start[min(tick, CHUNKS - 1)]
        if tick > 0:
            inbox = jnp.where(stage == 0, inbox, received)
        slot = tick - stage
        slot = jnp.where((slot >= 0) & (slot < CHUNKS), slot, CHUNKS)
        spread = jnp.broadcast_to(inbox[None], (tiles, wide, rows))
        for layer in range(CORES * layers):
            own, half = layer % layers, layer // layers
            full = to_all(spread)
            if tick == 0 and layer < layers:
                others = (narrow(arrived[layer], layer, layers, others + (spread,) * layer),)
            spread = layer_step(core_arg, full, whole, interface, others[0], half, own, layer)
            place = (half, slot, 0, 0, 0)
            saved[own] = lax.dynamic_update_slice(saved[own], full[None, None], place)
            place = (half, slot, tiles, 0, 0)
            saved[own] = lax.dynamic_update_slice(saved[own], spread[None, None, :1], place)
        received = lax.ppermute(spread[0], "layer", ring)

    finish(0)
    finish(1)
    return fields[0], jnp.stack(leaving)


def solution(mesh):
    in_specs = (
        P("tile", None),
        P("layer", "tile", None),
        P("layer", "tile", None),
        P("layer", None),
        P("layer", None),
    )
    out_specs = (P("layer", "tile", None), P("layer", "tile", None))
    return jax.shard_map(
        on_device, mesh=mesh, in_specs=in_specs, out_specs=out_specs, check_vma=False
    )
```

```python
import functools

import jax
import jax.numpy as jnp
from jax import lax
from jax.experimental import pallas as pl
from jax.experimental.pallas import tpu as pltpu
from jax.sharding import PartitionSpec as P

DEPTHS = 4
CHUNKS = 2
CORES = 2
PARTS = 2
PIECES = 4
GATHERED = 2
SLOTS = 32
NT = (((1,), (1,)), ((), ()))
VMEM = pl.BlockSpec(memory_space=pltpu.VMEM)
SMEM = pl.BlockSpec(memory_space=pltpu.SMEM)
ANYWHERE = pl.BlockSpec(memory_space=pl.ANY)
PARAMS = pltpu.CompilerParams(vmem_limit_bytes=48 * 1024 * 1024)


def widen_kernel(mat_ref, after_ref, out_ref):
    out_ref[...] = mat_ref[0].astype(jnp.float32)


def widen(mats, layer, part, after):
    rows, orders = mats.shape[1:]
    height = rows // PARTS
    piece = height // PIECES
    return pl.pallas_call(
        widen_kernel,
        out_shape=jax.ShapeDtypeStruct((height, orders), jnp.float32),
        grid=(PIECES,),
        in_specs=[
            pl.BlockSpec((1, piece, orders), lambda p: (layer, part * PIECES + p, 0)),
            ANYWHERE,
        ],
        out_specs=pl.BlockSpec((piece, orders), lambda p: (p, 0)),
        compiler_params=PARAMS,
    )(mats, after)


def narrow_kernel(mat_ref, *refs):
    refs[-1][0] = mat_ref[...].astype(jnp.bfloat16)


def narrow(mat, layer, part, layers, before):
    height, orders = mat.shape
    piece = height // PIECES
    return pl.pallas_call(
        narrow_kernel,
        out_shape=jax.ShapeDtypeStruct((layers, height * PARTS, orders), jnp.bfloat16),
        grid=(PIECES,),
        in_specs=[pl.BlockSpec((piece, orders), lambda p: (p, 0))] + [ANYWHERE] * len(before),
        out_specs=pl.BlockSpec((1, piece, orders), lambda p: (layer, part * PIECES + p, 0)),
        input_output_aliases={1: 0} if before else {},
        compiler_params=PARAMS,
    )(mat, *before)


def step_kernel(
    plan_ref, full_ref, phase_ref, own_ref, other_ref, saved_in,
    out_ref, saved_ref, row_buf, mat_buf, sum_buf, row_sem, sems, save_sems,
    *, tick, half, layer, number
):
    blocks, wide, rows = full_ref.shape
    split = wide // 2
    core, valid, slot = plan_ref[tick, 0], plan_ref[tick, 1], plan_ref[tick, 2 + number]
    row_copy = pltpu.make_async_copy(phase_ref.at[number], row_buf, row_sem)
    row_copy.start()

    def copies(mats_ref):
        return [
            pltpu.make_async_copy(
                mats_ref.at[layer, :, pl.ds(b * rows, rows)], mat_buf.at[b], sems.at[b]
            )
            for b in range(blocks)
        ]

    @pl.when(core == half)
    def _():
        for copy in copies(own_ref):
            copy.start()

    @pl.when(core != half)
    def _():
        for copy in copies(other_ref):
            copy.start()

    block_save = pltpu.make_async_copy(
        full_ref, saved_ref.at[slot, pl.ds(0, blocks)], save_sems.at[0]
    )
    sum_save = pltpu.make_async_copy(sum_buf, saved_ref.at[slot, blocks], save_sems.at[1])

    @pl.when(valid == 1)
    def _():
        block_save.start()

    arrivals = copies(own_ref)
    total = jnp.zeros((wide, rows), jnp.float32)
    row_copy.wait()
    for b in range(blocks):
        cosine = row_buf[0, b : b + 1, :]
        sine = row_buf[1, b : b + 1, :]
        real_part = full_ref[b, :split, :]
        imag_part = full_ref[b, split:, :]
        phased = jnp.concatenate(
            [cosine * real_part - sine * imag_part, sine * real_part + cosine * imag_part], axis=0
        ).astype(jnp.bfloat16)
        arrivals[b].wait()
        total += lax.dot_general(phased, mat_buf[b], NT, preferred_element_type=jnp.float32)
    sum_buf[...] = total


    @pl.when(valid == 1)
    def _():
        sum_save.start()

    for b in range(blocks):
        out_ref[b] = total

    @pl.when(valid == 1)
    def _():
        block_save.wait()
        sum_save.wait()


def allocate_kernel(out_ref):
    pass


def allocate(shape):
    return pl.pallas_call(
        allocate_kernel,
        out_shape=jax.ShapeDtypeStruct(shape, jnp.float32),
        in_specs=[],
        out_specs=ANYWHERE,
        compiler_params=PARAMS,
    )()


def layer_step(plan, full, phases, own, other, saved, tick, half, layer, number):
    blocks, wide, rows = full.shape
    return pl.pallas_call(
        functools.partial(
            step_kernel, tick=tick, half=half, layer=layer, number=number
        ),
        out_shape=(
            jax.ShapeDtypeStruct(full.shape, jnp.float32),
            jax.ShapeDtypeStruct(saved.shape, jnp.float32),
        ),
        in_specs=[SMEM, VMEM] + [ANYWHERE] * 4,
        out_specs=(VMEM, ANYWHERE),
        input_output_aliases={5: 1},
        scratch_shapes=[
            pltpu.VMEM(phases.shape[1:], jnp.float32),
            pltpu.VMEM((blocks, rows, rows), jnp.bfloat16),
            pltpu.VMEM((wide, rows), jnp.float32),
            pltpu.SemaphoreType.DMA,
            pltpu.SemaphoreType.DMA((blocks,)),
            pltpu.SemaphoreType.DMA((2,)),
        ],
        compiler_params=PARAMS,
        cost_estimate=pl.CostEstimate(
            flops=2 * wide * rows * rows * blocks,
            bytes_accessed=2 * blocks * rows * rows,
            transcendentals=0,
        ),
    )(plan, full, phases, own, other, saved)


def fields_kernel(
    core_ref, own_ref, other_ref, own_leave_ref, other_leave_ref, cos_ref, sin_ref, mat_ref, *refs
):
    out_ref, leave_ref, total = refs[-3:]
    step = pl.program_id(0)
    chunks, gathered, wide, rows = other_ref.shape
    half = wide // 2
    first = core_ref[0] == 0

    def columns(mine_ref, theirs_ref, b, part):
        mine = mine_ref[:, b, part, :].reshape(chunks * half, rows)
        theirs = theirs_ref[:, b, part, :].reshape(chunks * half, rows)
        low = jnp.where(first, mine, theirs)
        high = jnp.where(first, theirs, mine)
        return jnp.concatenate([low, high], axis=0)

    spans = []
    for b in range(gathered):
        real_part = columns(own_ref, other_ref, b, slice(0, half))
        imag_part = columns(own_ref, other_ref, b, slice(half, wide))
        parts = [real_part.astype(jnp.bfloat16), imag_part.astype(jnp.bfloat16)]
        for depth in range(DEPTHS - 1):
            cosine = cos_ref[b, depth : depth + 1, :]
            sine = sin_ref[b, depth : depth + 1, :]
            parts.append((cosine * real_part - sine * imag_part).astype(jnp.bfloat16))
            parts.append((sine * real_part + cosine * imag_part).astype(jnp.bfloat16))
        spans.append(jnp.concatenate(parts, axis=0))
    depths = jnp.concatenate(spans, axis=1)
    partial = lax.dot_general(mat_ref[0], depths, NT, preferred_element_type=jnp.float32)

    @pl.when(step == 0)
    def _():
        total[...] = partial
        leave = [
            columns(own_leave_ref, other_leave_ref, 0, part)
            for part in (slice(0, half), slice(half, wide))
        ]
        leave_ref[0] = jnp.concatenate(leave, axis=0).T

    @pl.when((step > 0) & (step < pl.num_programs(0) - 1))
    def _():
        total[...] += partial

    @pl.when(step == pl.num_programs(0) - 1)
    def _():
        out_ref[0] = (total[...] + partial).astype(jnp.bfloat16)


def layer_fields(core, own, other, cosines, sines, eigvec, layer, before):
    chunks, blocks, wide, rows = other.shape
    layers, _, orders = eigvec.shape
    blocks -= 1
    width = CORES * chunks * wide
    cols = DEPTHS * width
    entering = pl.BlockSpec((chunks, GATHERED, wide, rows), lambda b, c: (0, b, 0, 0))
    leave = pl.BlockSpec((chunks, 1, wide, rows), lambda b, c: (0, blocks, 0, 0))
    own_entering = pl.BlockSpec(
        (chunks, GATHERED, wide, rows), lambda b, c: (layer * CORES, b, 0, 0)
    )
    own_leave = pl.BlockSpec((chunks, 1, wide, rows), lambda b, c: (layer * CORES, blocks, 0, 0))
    coef = pl.BlockSpec((GATHERED, DEPTHS, rows), lambda b, c: (b, 0, 0))
    return pl.pallas_call(
        fields_kernel,
        out_shape=(
            jax.ShapeDtypeStruct((layers, rows, cols), jnp.bfloat16),
            jax.ShapeDtypeStruct((layers, rows, width), jnp.float32),
        ),
        grid_spec=pltpu.PrefetchScalarGridSpec(
            num_scalar_prefetch=1,
            grid=(blocks // GATHERED,),
            in_specs=[
                own_entering,
                entering,
                own_leave,
                leave,
                coef,
                coef,
                pl.BlockSpec((1, rows, rows * GATHERED), lambda b, c: (layer, 0, b)),
            ]
            + [ANYWHERE] * len(before),
            out_specs=(
                pl.BlockSpec((1, rows, cols), lambda b, c: (layer, 0, 0)),
                pl.BlockSpec((1, rows, width), lambda b, c: (layer, 0, 0)),
            ),
            scratch_shapes=[pltpu.VMEM((rows, cols), jnp.float32)],
        ),
        input_output_aliases={8: 0, 9: 1} if before else {},
        compiler_params=PARAMS,
    )(core, own, other, own, other, cosines, sines, eigvec, *before)


def to_all(block):
    return lax.all_to_all(block, "tile", split_axis=0, concat_axis=0, tiled=False)


def on_device(incident, interface, eigvec, angle, decay):
    groups = lax.axis_size("layer")
    tiles = lax.axis_size("tile")
    member = lax.axis_index("layer")
    core = (member % CORES).astype(jnp.int32)
    stage = (member // CORES).astype(jnp.int32)
    stages = groups // CORES
    layers, rows, orders = interface.shape
    width = incident.shape[1]
    part = width // 2 // CORES // CHUNKS
    wide = 2 * part
    partner = [(i, i ^ 1) for i in range(groups)]
    ring = [(i, (i + CORES) % groups) for i in range(groups)]

    phases = jnp.stack([angle, decay]).reshape(2, layers, tiles, rows)
    other_phases = lax.ppermute(phases, "layer", partner)
    after = incident
    arrived = []
    for layer in range(layers):
        arrived.append([])
        for piece in range(PARTS):
            after = widen(interface, layer, piece, after)
            arrived[layer].append(lax.ppermute(after, "layer", partner))
    others = ()
    early = jnp.where(core == 0, phases, other_phases)
    late = jnp.where(core == 0, other_phases, phases)
    all_phases = jnp.concatenate([early, late], axis=1)
    scale = jnp.exp(-all_phases[1])
    whole = jnp.stack([scale * jnp.cos(all_phases[0]), scale * jnp.sin(all_phases[0])], axis=1)
    fracs = (jnp.arange(1, DEPTHS + 1, dtype=jnp.float32) / DEPTHS).reshape(1, 1, DEPTHS, 1)
    scale = jnp.exp(-fracs * phases[1][:, :, None, :])
    cosines = scale * jnp.cos(fracs * phases[0][:, :, None, :])
    sines = scale * jnp.sin(fracs * phases[0][:, :, None, :])

    whole, cosines, sines = lax.optimization_barrier((whole, cosines, sines))

    start = incident.astype(jnp.float32).T.reshape(2, CORES, CHUNKS, part, rows)
    start = jnp.where(core == 0, start[:, 0], start[:, 1])
    start = start.transpose(1, 0, 2, 3).reshape(CHUNKS, wide, rows)

    ticks = jnp.arange(stages + CHUNKS - 1, dtype=jnp.int32)
    slots = ticks - stage
    valid = (slots >= 0) & (slots < CHUNKS)
    slots = jnp.clip(slots, 0, CHUNKS - 1)
    plan = [jnp.full_like(ticks, core), valid.astype(jnp.int32)]
    for number in range(CORES * layers):
        kind = (core != number // layers).astype(jnp.int32)
        plan.append((number % layers * CORES + kind) * CHUNKS + slots)
    plan = jnp.stack(plan, axis=1)

    saved = allocate((SLOTS, tiles + 1, wide, rows))
    received = None
    for tick in range(stages + CHUNKS - 1):
        inbox = start[min(tick, CHUNKS - 1)]
        if tick > 0:
            inbox = jnp.where(stage == 0, inbox, received)
        spread = jnp.broadcast_to(inbox[None], (tiles, wide, rows))
        for number in range(CORES * layers):
            own, half = number % layers, number // layers
            full = to_all(spread)
            if tick == 0 and number < layers:
                for piece in range(PARTS):
                    tied = others + (spread,) * min(number, 1)
                    others = (narrow(arrived[own][piece], own, piece, layers, tied),)
            spread, saved = layer_step(
                plan, full, whole, interface, others[0], saved, tick, half, own, number
            )
        received = lax.ppermute(spread[0], "layer", ring)

    results = ()
    for layer in range(layers):
        first = (layer * CORES + 1) * CHUNKS
        other = lax.ppermute(saved[first : first + CHUNKS], "layer", partner)
        results = layer_fields(
            core.reshape(1), saved, other, cosines[layer], sines[layer], eigvec, layer,
            results,
        )
    return results


def solution(mesh):
    in_specs = (
        P("tile", None),
        P("layer", "tile", None),
        P("layer", "tile", None),
        P("layer", None),
        P("layer", None),
    )
    out_specs = (P("layer", "tile", None), P("layer", "tile", None))
    return jax.shard_map(
        on_device, mesh=mesh, in_specs=in_specs, out_specs=out_specs, check_vma=False
    )
```

```python
import functools

import jax
import jax.numpy as jnp
from jax import lax
from jax.experimental import pallas as pl
from jax.experimental.pallas import tpu as pltpu
from jax.sharding import PartitionSpec as P

DEPTHS = 4
CHUNKS = 2
CORES = 2
PARTS = 2
PIECES = 2
GATHERED = 4
SLOTS = 32
NT = (((1,), (1,)), ((), ()))
VMEM = pl.BlockSpec(memory_space=pltpu.VMEM)
SMEM = pl.BlockSpec(memory_space=pltpu.SMEM)
ANYWHERE = pl.BlockSpec(memory_space=pl.ANY)
PARAMS = pltpu.CompilerParams(vmem_limit_bytes=48 * 1024 * 1024)


def widen_kernel(mat_ref, after_ref, out_ref):
    out_ref[...] = mat_ref[0].astype(jnp.float32)


def widen(mats, layer, part, after):
    rows, orders = mats.shape[1:]
    height = rows // PARTS
    piece = height // PIECES
    return pl.pallas_call(
        widen_kernel,
        out_shape=jax.ShapeDtypeStruct((height, orders), jnp.float32),
        grid=(PIECES,),
        in_specs=[
            pl.BlockSpec((1, piece, orders), lambda p: (layer, part * PIECES + p, 0)),
            ANYWHERE,
        ],
        out_specs=pl.BlockSpec((piece, orders), lambda p: (p, 0)),
        compiler_params=PARAMS,
    )(mats, after)


def narrow_kernel(mat_ref, *refs):
    refs[-1][0] = mat_ref[...].astype(jnp.bfloat16)


def narrow(mat, layer, part, layers, before):
    height, orders = mat.shape
    piece = height // PIECES
    return pl.pallas_call(
        narrow_kernel,
        out_shape=jax.ShapeDtypeStruct((layers, height * PARTS, orders), jnp.bfloat16),
        grid=(PIECES,),
        in_specs=[pl.BlockSpec((piece, orders), lambda p: (p, 0))] + [ANYWHERE] * len(before),
        out_specs=pl.BlockSpec((1, piece, orders), lambda p: (layer, part * PIECES + p, 0)),
        input_output_aliases={1: 0} if before else {},
        compiler_params=PARAMS,
    )(mat, *before)


def step_kernel(
    full_ref, phase_ref, own_ref, other_ref, saved_in, *refs, tick, number, layers, ticks
):
    out_ref, saved_ref, row_buf, mat_buf, sum_buf, row_sem, sems, save_sems = refs[-8:]
    blocks, wide, rows = full_ref.shape
    split = wide // 2
    half, layer = number // layers, number % layers
    member = lax.axis_index("layer")
    core = lax.rem(member, CORES)
    stage = lax.div(member, CORES)
    left = CORES * layers - 1 - number
    late = tick == ticks - 1 and left < 2
    behind = (tick or number) and not (late and left == 0)
    row_copy = pltpu.make_async_copy(phase_ref.at[number], row_buf, row_sem)
    row_copy.start()

    def copies(mats_ref):
        return [
            pltpu.make_async_copy(
                mats_ref.at[layer, :, pl.ds(b * rows, rows)], mat_buf.at[b], sems.at[b]
            )
            for b in range(blocks)
        ]

    @pl.when(core == half)
    def _():
        for copy in copies(own_ref):
            copy.start()

    @pl.when(core != half)
    def _():
        for copy in copies(other_ref):
            copy.start()

    def chunk_of(tick):
        return (tick >= stage) & (tick - stage < CHUNKS), jnp.clip(tick - stage, 0, CHUNKS - 1)

    def entry(number, chunk):
        kind = jnp.where(core == number // layers, 0, 1)
        return (number % layers * CORES + kind) * CHUNKS + chunk

    valid, chunk = chunk_of(tick)
    block_save = pltpu.make_async_copy(
        full_ref, saved_ref.at[entry(number, chunk), pl.ds(0, blocks)], save_sems.at[0]
    )
    if behind:
        before = (number - 1) % (CORES * layers)
        before_valid, before_chunk = chunk_of(tick - (number == 0))
        before_save = pltpu.make_async_copy(
            refs[0].at[0], saved_ref.at[entry(before, before_chunk), blocks], save_sems.at[1]
        )

    @pl.when(valid)
    def _():
        block_save.start()

    if behind:

        @pl.when(before_valid)
        def _():
            before_save.start()

    arrivals = copies(own_ref)
    total = jnp.zeros((wide, rows), jnp.float32)
    row_copy.wait()
    for b in range(blocks):
        cosine = row_buf[0, b : b + 1, :]
        sine = row_buf[1, b : b + 1, :]
        real_part = full_ref[b, :split, :]
        imag_part = full_ref[b, split:, :]
        phased = jnp.concatenate(
            [cosine * real_part - sine * imag_part, sine * real_part + cosine * imag_part], axis=0
        ).astype(jnp.bfloat16)
        arrivals[b].wait()
        total += lax.dot_general(phased, mat_buf[b], NT, preferred_element_type=jnp.float32)

    for b in range(blocks):
        out_ref[b] = total

    if late:
        sum_buf[...] = total
        sum_save = pltpu.make_async_copy(
            sum_buf, saved_ref.at[entry(number, chunk), blocks], save_sems.at[2]
        )

        @pl.when(valid)
        def _():
            sum_save.start()
            sum_save.wait()

    @pl.when(valid)
    def _():
        block_save.wait()

    if behind:

        @pl.when(before_valid)
        def _():
            before_save.wait()


def allocate_kernel(out_ref):
    pass


def allocate(shape):
    return pl.pallas_call(
        allocate_kernel,
        out_shape=jax.ShapeDtypeStruct(shape, jnp.float32),
        in_specs=[],
        out_specs=ANYWHERE,
        compiler_params=PARAMS,
    )()


def layer_step(full, phases, own, other, saved, extra, **place):
    blocks, wide, rows = full.shape
    return pl.pallas_call(
        functools.partial(step_kernel, **place),
        out_shape=(
            jax.ShapeDtypeStruct(full.shape, jnp.float32),
            jax.ShapeDtypeStruct(saved.shape, jnp.float32),
        ),
        in_specs=[VMEM] + [ANYWHERE] * (4 + len(extra)),
        out_specs=(VMEM, ANYWHERE),
        input_output_aliases={4: 1},
        scratch_shapes=[
            pltpu.VMEM(phases.shape[1:], jnp.float32),
            pltpu.VMEM((blocks, rows, rows), jnp.bfloat16),
            pltpu.VMEM((wide, rows), jnp.float32),
            pltpu.SemaphoreType.DMA,
            pltpu.SemaphoreType.DMA((blocks,)),
            pltpu.SemaphoreType.DMA((3,)),
        ],
        compiler_params=PARAMS,
        cost_estimate=pl.CostEstimate(
            flops=2 * wide * rows * rows * blocks,
            bytes_accessed=2 * blocks * rows * rows,
            transcendentals=0,
        ),
    )(full, phases, own, other, saved, *extra)


def fields_kernel(
    core_ref, own_ref, other_ref, own_leave_ref, other_leave_ref, cos_ref, sin_ref, mat_ref, *refs
):
    out_ref, leave_ref, total = refs[-3:]
    step = pl.program_id(0)
    chunks, gathered, wide, rows = other_ref.shape
    half = wide // 2
    first = core_ref[0] == 0

    def columns(mine_ref, theirs_ref, b, part):
        mine = mine_ref[:, b, part, :].reshape(chunks * half, rows)
        theirs = theirs_ref[:, b, part, :].reshape(chunks * half, rows)
        low = jnp.where(first, mine, theirs)
        high = jnp.where(first, theirs, mine)
        return jnp.concatenate([low, high], axis=0)

    spans = []
    for b in range(gathered):
        real_part = columns(own_ref, other_ref, b, slice(0, half))
        imag_part = columns(own_ref, other_ref, b, slice(half, wide))
        parts = [real_part.astype(jnp.bfloat16), imag_part.astype(jnp.bfloat16)]
        for depth in range(DEPTHS - 1):
            cosine = cos_ref[b, depth : depth + 1, :]
            sine = sin_ref[b, depth : depth + 1, :]
            parts.append((cosine * real_part - sine * imag_part).astype(jnp.bfloat16))
            parts.append((sine * real_part + cosine * imag_part).astype(jnp.bfloat16))
        spans.append(jnp.concatenate(parts, axis=0))
    depths = jnp.concatenate(spans, axis=1)
    partial = lax.dot_general(mat_ref[0], depths, NT, preferred_element_type=jnp.float32)

    @pl.when(step == 0)
    def _():
        total[...] = partial
        leave = [
            columns(own_leave_ref, other_leave_ref, 0, part)
            for part in (slice(0, half), slice(half, wide))
        ]
        leave_ref[0] = jnp.concatenate(leave, axis=0).T

    @pl.when((step > 0) & (step < pl.num_programs(0) - 1))
    def _():
        total[...] += partial

    @pl.when(step == pl.num_programs(0) - 1)
    def _():
        out_ref[0] = (total[...] + partial).astype(jnp.bfloat16)


def layer_fields(core, own, other, cosines, sines, eigvec, layer, before):
    chunks, blocks, wide, rows = other.shape
    layers, _, orders = eigvec.shape
    blocks -= 1
    width = CORES * chunks * wide
    cols = DEPTHS * width
    entering = pl.BlockSpec((chunks, GATHERED, wide, rows), lambda b, c: (0, b, 0, 0))
    leave = pl.BlockSpec((chunks, 1, wide, rows), lambda b, c: (0, blocks, 0, 0))
    own_entering = pl.BlockSpec(
        (chunks, GATHERED, wide, rows), lambda b, c: (layer * CORES, b, 0, 0)
    )
    own_leave = pl.BlockSpec((chunks, 1, wide, rows), lambda b, c: (layer * CORES, blocks, 0, 0))
    coef = pl.BlockSpec((GATHERED, DEPTHS, rows), lambda b, c: (b, 0, 0))
    return pl.pallas_call(
        fields_kernel,
        out_shape=(
            jax.ShapeDtypeStruct((layers, rows, cols), jnp.bfloat16),
            jax.ShapeDtypeStruct((layers, rows, width), jnp.float32),
        ),
        grid_spec=pltpu.PrefetchScalarGridSpec(
            num_scalar_prefetch=1,
            grid=(blocks // GATHERED,),
            in_specs=[
                own_entering,
                entering,
                own_leave,
                leave,
                coef,
                coef,
                pl.BlockSpec((1, rows, rows * GATHERED), lambda b, c: (layer, 0, b)),
            ]
            + [ANYWHERE] * len(before),
            out_specs=(
                pl.BlockSpec((1, rows, cols), lambda b, c: (layer, 0, 0)),
                pl.BlockSpec((1, rows, width), lambda b, c: (layer, 0, 0)),
            ),
            scratch_shapes=[pltpu.VMEM((rows, cols), jnp.float32)],
        ),
        input_output_aliases={8: 0, 9: 1} if before else {},
        compiler_params=PARAMS,
    )(core, own, other, own, other, cosines, sines, eigvec, *before)


def to_all(block):
    return lax.all_to_all(block, "tile", split_axis=0, concat_axis=0, tiled=False)


def on_device(incident, interface, eigvec, angle, decay):
    groups = lax.axis_size("layer")
    tiles = lax.axis_size("tile")
    member = lax.axis_index("layer")
    core = (member % CORES).astype(jnp.int32)
    stage = (member // CORES).astype(jnp.int32)
    stages = groups // CORES
    layers, rows, orders = interface.shape
    width = incident.shape[1]
    part = width // 2 // CORES // CHUNKS
    wide = 2 * part
    partner = [(i, i ^ 1) for i in range(groups)]
    ring = [(i, (i + CORES) % groups) for i in range(groups)]

    phases = jnp.stack([angle, decay]).reshape(2, layers, tiles, rows)
    other_phases = lax.ppermute(phases, "layer", partner)
    def swap(layer, after):
        pieces = []
        for piece in range(PARTS):
            after = widen(interface, layer, piece, after)
            pieces.append(lax.ppermute(after, "layer", partner))
        return pieces, after

    arrived = [swap(0, incident)[0]]
    others = ()
    early = jnp.where(core == 0, phases, other_phases)
    late = jnp.where(core == 0, other_phases, phases)
    all_phases = jnp.concatenate([early, late], axis=1)
    scale = jnp.exp(-all_phases[1])
    whole = jnp.stack([scale * jnp.cos(all_phases[0]), scale * jnp.sin(all_phases[0])], axis=1)
    fracs = (jnp.arange(1, DEPTHS + 1, dtype=jnp.float32) / DEPTHS).reshape(1, 1, DEPTHS, 1)
    scale = jnp.exp(-fracs * phases[1][:, :, None, :])
    cosines = scale * jnp.cos(fracs * phases[0][:, :, None, :])
    sines = scale * jnp.sin(fracs * phases[0][:, :, None, :])

    whole, cosines, sines = lax.optimization_barrier((whole, cosines, sines))

    start = incident.astype(jnp.float32).T.reshape(2, CORES, CHUNKS, part, rows)
    start = jnp.where(core == 0, start[:, 0], start[:, 1])
    start = start.transpose(1, 0, 2, 3).reshape(CHUNKS, wide, rows)

    ticks = stages + CHUNKS - 1
    saved = allocate((SLOTS, tiles + 1, wide, rows))
    results = ()

    def finish(layer):
        first = (layer * CORES + 1) * CHUNKS
        other = lax.ppermute(saved[first : first + CHUNKS], "layer", partner)
        return layer_fields(
            core.reshape(1), saved, other, cosines[layer], sines[layer], eigvec, layer, results
        )

    received = None
    computed = ()
    for tick in range(ticks):
        inbox = start[min(tick, CHUNKS - 1)]
        if tick > 0:
            inbox = jnp.where(stage == 0, inbox, received)
        spread = jnp.broadcast_to(inbox[None], (tiles, wide, rows))
        for number in range(CORES * layers):
            full = to_all(spread)
            if tick == 0 and number < layers:
                for piece in range(PARTS):
                    tied = others + (spread,) * min(number, 1)
                    if number == 0 and piece == 0:
                        after = whole
                        for later in range(1, layers):
                            pieces, after = swap(later, after)
                            arrived.append(pieces)
                    others = (narrow(arrived[number][piece], number, piece, layers, tied),)
            if tick == ticks - 1 and number == CORES * layers - 1:
                results = finish(0)
                computed += tuple(results[1:])
            spread, saved = layer_step(
                full, whole, interface, others[0], saved, computed,
                tick=tick, number=number, layers=layers, ticks=ticks,
            )
            computed = (spread,)
        received = lax.ppermute(spread[0], "layer", ring)

    for layer in range(1, layers):
        results = finish(layer)
    return results


def solution(mesh):
    in_specs = (
        P("tile", None),
        P("layer", "tile", None),
        P("layer", "tile", None),
        P("layer", None),
        P("layer", None),
    )
    out_specs = (P("layer", "tile", None), P("layer", "tile", None))
    return jax.shard_map(
        on_device, mesh=mesh, in_specs=in_specs, out_specs=out_specs, check_vma=False
    )
```

```python
import functools

import jax
import jax.numpy as jnp
from jax import lax
from jax.experimental import pallas as pl
from jax.experimental.pallas import tpu as pltpu
from jax.sharding import PartitionSpec as P

DEPTHS = 4
CHUNKS = 2
CORES = 2
PARTS = 2
PIECES = 2
GATHERED = 4
SLOTS = 48
NT = (((1,), (1,)), ((), ()))
VMEM = pl.BlockSpec(memory_space=pltpu.VMEM)
SMEM = pl.BlockSpec(memory_space=pltpu.SMEM)
ANYWHERE = pl.BlockSpec(memory_space=pl.ANY)
STEP_PARAMS = pltpu.CompilerParams(vmem_limit_bytes=36 * 1024 * 1024)
PARAMS = pltpu.CompilerParams(vmem_limit_bytes=48 * 1024 * 1024)


def widen_kernel(mat_ref, after_ref, out_ref):
    out_ref[...] = mat_ref[0].astype(jnp.float32)


def widen(mats, layer, part, after):
    rows, orders = mats.shape[1:]
    height = rows // PARTS
    piece = height // PIECES
    return pl.pallas_call(
        widen_kernel,
        out_shape=jax.ShapeDtypeStruct((height, orders), jnp.float32),
        grid=(PIECES,),
        in_specs=[
            pl.BlockSpec((1, piece, orders), lambda p: (layer, part * PIECES + p, 0)),
            ANYWHERE,
        ],
        out_specs=pl.BlockSpec((piece, orders), lambda p: (p, 0)),
        compiler_params=PARAMS,
    )(mats, after)


def place_kernel(own_ref, other_ref, *refs, half):
    core = lax.rem(lax.axis_index("layer"), CORES)
    refs[-1][...] = jnp.where(core == half, own_ref[0], other_ref[...].astype(jnp.bfloat16))


def place(mats, other, layer, part, half, before):
    height, orders = other.shape
    piece = height // PIECES
    aliased = part > 0
    return pl.pallas_call(
        functools.partial(place_kernel, half=half),
        out_shape=jax.ShapeDtypeStruct((height * PARTS, orders), jnp.bfloat16),
        grid=(PIECES,),
        in_specs=[
            pl.BlockSpec((1, piece, orders), lambda p: (layer, part * PIECES + p, 0)),
            pl.BlockSpec((piece, orders), lambda p: (p, 0)),
        ]
        + [ANYWHERE] * len(before),
        out_specs=pl.BlockSpec((piece, orders), lambda p: (part * PIECES + p, 0)),
        input_output_aliases={2: 0} if aliased else {},
        compiler_params=PARAMS,
    )(mats, other, *before)


def step_kernel(
    full_ref, phase_ref, mat_ref, saved_in, *refs, tick, number, layers, ticks
):
    out_ref, saved_ref, sum_buf, save_sems = refs[-4:]
    blocks, wide, rows = full_ref.shape
    split = wide // 2
    member = lax.axis_index("layer")
    core = lax.rem(member, CORES)
    stage = lax.div(member, CORES)
    left = CORES * layers - 1 - number
    late = tick == ticks - 1 and left < 2
    behind = (tick or number) and not (late and left == 0)
    def chunk_of(tick):
        return (tick >= stage) & (tick - stage < CHUNKS), jnp.clip(tick - stage, 0, CHUNKS - 1)

    def entry(number, chunk):
        kind = jnp.where(core == number // layers, 0, 1)
        return (number % layers * CORES + kind) * CHUNKS + chunk

    valid, chunk = chunk_of(tick)
    block_save = pltpu.make_async_copy(
        full_ref, saved_ref.at[entry(number, chunk), pl.ds(0, blocks)], save_sems.at[0]
    )
    if behind:
        before = (number - 1) % (CORES * layers)
        before_valid, before_chunk = chunk_of(tick - (number == 0))
        before_save = pltpu.make_async_copy(
            refs[0].at[0], saved_ref.at[entry(before, before_chunk), blocks], save_sems.at[1]
        )

    @pl.when(valid)
    def _():
        block_save.start()

    if behind:

        @pl.when(before_valid)
        def _():
            before_save.start()

    total = jnp.zeros((wide, rows), jnp.float32)
    for b in range(blocks):
        cosine = phase_ref[number, 0, b : b + 1, :]
        sine = phase_ref[number, 1, b : b + 1, :]
        real_part = full_ref[b, :split, :]
        imag_part = full_ref[b, split:, :]
        phased = jnp.concatenate(
            [cosine * real_part - sine * imag_part, sine * real_part + cosine * imag_part], axis=0
        ).astype(jnp.bfloat16)
        mat = mat_ref[:, b * rows : (b + 1) * rows]
        total += lax.dot_general(phased, mat, NT, preferred_element_type=jnp.float32)

    for b in range(blocks):
        out_ref[b] = total

    if late:
        sum_buf[...] = total
        sum_save = pltpu.make_async_copy(
            sum_buf, saved_ref.at[entry(number, chunk), blocks], save_sems.at[2]
        )

        @pl.when(valid)
        def _():
            sum_save.start()
            sum_save.wait()

    @pl.when(valid)
    def _():
        block_save.wait()

    if behind:

        @pl.when(before_valid)
        def _():
            before_save.wait()


def allocate_kernel(out_ref):
    pass


def allocate(shape):
    return pl.pallas_call(
        allocate_kernel,
        out_shape=jax.ShapeDtypeStruct(shape, jnp.float32),
        in_specs=[],
        out_specs=ANYWHERE,
        compiler_params=PARAMS,
    )()


def layer_step(full, phases, mat, saved, extra, **position):
    blocks, wide, rows = full.shape
    return pl.pallas_call(
        functools.partial(step_kernel, **position),
        out_shape=(
            jax.ShapeDtypeStruct(full.shape, jnp.float32),
            jax.ShapeDtypeStruct(saved.shape, jnp.float32),
        ),
        in_specs=[VMEM] * 3 + [ANYWHERE] * (1 + len(extra)),
        out_specs=(VMEM, ANYWHERE),
        input_output_aliases={3: 1},
        scratch_shapes=[
            pltpu.VMEM((wide, rows), jnp.float32),
            pltpu.SemaphoreType.DMA((3,)),
        ],
        compiler_params=STEP_PARAMS,
        cost_estimate=pl.CostEstimate(
            flops=2 * wide * rows * rows * blocks,
            bytes_accessed=2 * blocks * rows * rows,
            transcendentals=0,
        ),
    )(full, phases, mat, saved, *extra)


def fields_kernel(
    core_ref, own_ref, other_ref, own_leave_ref, other_leave_ref, cos_ref, sin_ref, mat_ref, *refs
):
    out_ref, leave_ref, total = refs[-3:]
    step = pl.program_id(0)
    chunks, gathered, wide, rows = other_ref.shape
    half = wide // 2
    first = core_ref[0] == 0

    def columns(mine_ref, theirs_ref, b, part):
        mine = mine_ref[:, b, part, :].reshape(chunks * half, rows)
        theirs = theirs_ref[:, b, part, :].reshape(chunks * half, rows)
        low = jnp.where(first, mine, theirs)
        high = jnp.where(first, theirs, mine)
        return jnp.concatenate([low, high], axis=0)

    spans = []
    for b in range(gathered):
        real_part = columns(own_ref, other_ref, b, slice(0, half))
        imag_part = columns(own_ref, other_ref, b, slice(half, wide))
        parts = [real_part.astype(jnp.bfloat16), imag_part.astype(jnp.bfloat16)]
        for depth in range(DEPTHS - 1):
            cosine = cos_ref[b, depth : depth + 1, :]
            sine = sin_ref[b, depth : depth + 1, :]
            parts.append((cosine * real_part - sine * imag_part).astype(jnp.bfloat16))
            parts.append((sine * real_part + cosine * imag_part).astype(jnp.bfloat16))
        spans.append(jnp.concatenate(parts, axis=0))
    depths = jnp.concatenate(spans, axis=1)
    partial = lax.dot_general(mat_ref[0], depths, NT, preferred_element_type=jnp.float32)

    @pl.when(step == 0)
    def _():
        total[...] = partial
        leave = [
            columns(own_leave_ref, other_leave_ref, 0, part)
            for part in (slice(0, half), slice(half, wide))
        ]
        leave_ref[0] = jnp.concatenate(leave, axis=0).T

    @pl.when((step > 0) & (step < pl.num_programs(0) - 1))
    def _():
        total[...] += partial

    @pl.when(step == pl.num_programs(0) - 1)
    def _():
        out_ref[0] = (total[...] + partial).astype(jnp.bfloat16)


def layer_fields(core, own, other, cosines, sines, eigvec, layer, before):
    chunks, blocks, wide, rows = other.shape
    layers, _, orders = eigvec.shape
    blocks -= 1
    width = CORES * chunks * wide
    cols = DEPTHS * width
    entering = pl.BlockSpec((chunks, GATHERED, wide, rows), lambda b, c: (0, b, 0, 0))
    leave = pl.BlockSpec((chunks, 1, wide, rows), lambda b, c: (0, blocks, 0, 0))
    own_entering = pl.BlockSpec(
        (chunks, GATHERED, wide, rows), lambda b, c: (layer * CORES, b, 0, 0)
    )
    own_leave = pl.BlockSpec((chunks, 1, wide, rows), lambda b, c: (layer * CORES, blocks, 0, 0))
    coef = pl.BlockSpec((GATHERED, DEPTHS, rows), lambda b, c: (b, 0, 0))
    return pl.pallas_call(
        fields_kernel,
        out_shape=(
            jax.ShapeDtypeStruct((layers, rows, cols), jnp.bfloat16),
            jax.ShapeDtypeStruct((layers, rows, width), jnp.float32),
        ),
        grid_spec=pltpu.PrefetchScalarGridSpec(
            num_scalar_prefetch=1,
            grid=(blocks // GATHERED,),
            in_specs=[
                own_entering,
                entering,
                own_leave,
                leave,
                coef,
                coef,
                pl.BlockSpec((1, rows, rows * GATHERED), lambda b, c: (layer, 0, b)),
            ]
            + [ANYWHERE] * len(before),
            out_specs=(
                pl.BlockSpec((1, rows, cols), lambda b, c: (layer, 0, 0)),
                pl.BlockSpec((1, rows, width), lambda b, c: (layer, 0, 0)),
            ),
            scratch_shapes=[pltpu.VMEM((rows, cols), jnp.float32)],
        ),
        input_output_aliases={8: 0, 9: 1} if before else {},
        compiler_params=PARAMS,
    )(core, own, other, own, other, cosines, sines, eigvec, *before)


def to_all(block):
    return lax.all_to_all(block, "tile", split_axis=0, concat_axis=0, tiled=False)


def on_device(incident, interface, eigvec, angle, decay):
    groups = lax.axis_size("layer")
    tiles = lax.axis_size("tile")
    member = lax.axis_index("layer")
    core = (member % CORES).astype(jnp.int32)
    stage = (member // CORES).astype(jnp.int32)
    stages = groups // CORES
    layers, rows, orders = interface.shape
    width = incident.shape[1]
    part = width // 2 // CORES // CHUNKS
    wide = 2 * part
    partner = [(i, i ^ 1) for i in range(groups)]
    ring = [(i, (i + CORES) % groups) for i in range(groups)]

    phases = jnp.stack([angle, decay]).reshape(2, layers, tiles, rows)
    other_phases = lax.ppermute(phases, "layer", partner)
    def swap(layer, after):
        pieces = []
        for piece in range(PARTS):
            after = widen(interface, layer, piece, after)
            pieces.append(lax.ppermute(after, "layer", partner))
        return pieces, after

    arrived = [swap(0, incident)[0]]
    mats = {}
    early = jnp.where(core == 0, phases, other_phases)
    late = jnp.where(core == 0, other_phases, phases)
    all_phases = jnp.concatenate([early, late], axis=1)
    scale = jnp.exp(-all_phases[1])
    whole = jnp.stack([scale * jnp.cos(all_phases[0]), scale * jnp.sin(all_phases[0])], axis=1)
    fracs = (jnp.arange(1, DEPTHS + 1, dtype=jnp.float32) / DEPTHS).reshape(1, 1, DEPTHS, 1)
    scale = jnp.exp(-fracs * phases[1][:, :, None, :])
    cosines = scale * jnp.cos(fracs * phases[0][:, :, None, :])
    sines = scale * jnp.sin(fracs * phases[0][:, :, None, :])

    whole, cosines, sines = lax.optimization_barrier((whole, cosines, sines))

    start = incident.astype(jnp.float32).T.reshape(2, CORES, CHUNKS, part, rows)
    start = jnp.where(core == 0, start[:, 0], start[:, 1])
    start = start.transpose(1, 0, 2, 3).reshape(CHUNKS, wide, rows)

    ticks = stages + CHUNKS - 1
    saved = allocate((SLOTS, tiles + 1, wide, rows))
    results = ()

    def finish(layer):
        first = (layer * CORES + 1) * CHUNKS
        other = lax.ppermute(saved[first : first + CHUNKS], "layer", partner)
        return layer_fields(
            core.reshape(1), saved, other, cosines[layer], sines[layer], eigvec, layer, results
        )

    received = None
    computed = ()
    for tick in range(ticks):
        inbox = start[min(tick, CHUNKS - 1)]
        if tick > 0:
            inbox = jnp.where(stage == 0, inbox, received)
        spread = jnp.broadcast_to(inbox[None], (tiles, wide, rows))
        for number in range(CORES * layers):
            full = to_all(spread)
            if tick == 0:
                own, half = number % layers, number // layers
                mat = ()
                for piece in range(PARTS):
                    if number == 0 and piece == 0:
                        arrived += [swap(layer, whole)[0] for layer in range(1, layers)]
                    tied = mat + (spread,) * min(number, 1)
                    mat = (place(interface, arrived[own][piece], own, piece, half, tied),)
                mats[number] = mat[0]
            if tick == ticks - 1 and number == CORES * layers - 1:
                results = finish(0)
                computed += tuple(results[1:])
            spread, saved = layer_step(
                full, whole, mats[number], saved, computed,
                tick=tick, number=number, layers=layers, ticks=ticks,
            )
            computed = (spread,)
        received = lax.ppermute(spread[0], "layer", ring)

    for layer in range(1, layers):
        results = finish(layer)
    return results


def solution(mesh):
    in_specs = (
        P("tile", None),
        P("layer", "tile", None),
        P("layer", "tile", None),
        P("layer", None),
        P("layer", None),
    )
    out_specs = (P("layer", "tile", None), P("layer", "tile", None))
    return jax.shard_map(
        on_device, mesh=mesh, in_specs=in_specs, out_specs=out_specs, check_vma=False
    )
```

```python
import functools

import jax
import jax.numpy as jnp
from jax import lax
from jax.experimental import pallas as pl
from jax.experimental.pallas import tpu as pltpu
from jax.sharding import PartitionSpec as P

DEPTHS = 4
CHUNKS = 2
CORES = 2
PARTS = 2
PIECES = 2
GATHERED = 4
SLOTS = 48
NT = (((1,), (1,)), ((), ()))
VMEM = pl.BlockSpec(memory_space=pltpu.VMEM)
SMEM = pl.BlockSpec(memory_space=pltpu.SMEM)
ANYWHERE = pl.BlockSpec(memory_space=pl.ANY)
PLACE_PARAMS = pltpu.CompilerParams(vmem_limit_bytes=58 * 1024 * 1024)
STEP_PARAMS = pltpu.CompilerParams(vmem_limit_bytes=36 * 1024 * 1024)
PARAMS = pltpu.CompilerParams(vmem_limit_bytes=48 * 1024 * 1024)


def widen_kernel(mat_ref, *refs):
    refs[-1][...] = mat_ref[0].astype(jnp.float32)


def widen(mats, layer, part, after):
    rows, orders = mats.shape[1:]
    height = rows // PARTS
    piece = height // PIECES
    return pl.pallas_call(
        widen_kernel,
        out_shape=jax.ShapeDtypeStruct((height, orders), jnp.float32),
        grid=(PIECES,),
        in_specs=[
            pl.BlockSpec((1, piece, orders), lambda p: (layer, part * PIECES + p, 0)),
        ]
        + [ANYWHERE] * len(after),
        out_specs=pl.BlockSpec((piece, orders), lambda p: (p, 0)),
        compiler_params=PARAMS,
    )(mats, *after)


def place_kernel(own_ref, other_ref, *refs):
    early_ref, late_ref = refs[-2:]
    core = lax.rem(lax.axis_index("layer"), CORES)
    own = own_ref[0]
    other = other_ref[...].astype(jnp.bfloat16)

    @pl.when(core == 0)
    def _():
        early_ref[...] = own
        late_ref[...] = other

    @pl.when(core != 0)
    def _():
        early_ref[...] = other
        late_ref[...] = own


def place(mats, other, layer, part, before):
    height, orders = other.shape
    piece = height // PIECES
    out = jax.ShapeDtypeStruct((height * PARTS, orders), jnp.bfloat16)
    spec = pl.BlockSpec((piece, orders), lambda p: (part * PIECES + p, 0))
    return pl.pallas_call(
        place_kernel,
        out_shape=(out, out),
        grid=(PIECES,),
        in_specs=[
            pl.BlockSpec((1, piece, orders), lambda p: (layer, part * PIECES + p, 0)),
            pl.BlockSpec((piece, orders), lambda p: (p, 0)),
        ]
        + [ANYWHERE] * len(before),
        out_specs=(spec, spec),
        input_output_aliases={2: 0, 3: 1} if part > 0 else {},
        compiler_params=PLACE_PARAMS,
    )(mats, other, *before)


def step_kernel(
    full_ref, phase_ref, mat_ref, saved_in, *refs, tick, number, layers, ticks
):
    out_ref, saved_ref, sum_buf, save_sems = refs[-4:]
    blocks, wide, rows = full_ref.shape
    split = wide // 2
    member = lax.axis_index("layer")
    core = lax.rem(member, CORES)
    stage = lax.div(member, CORES)
    left = CORES * layers - 1 - number
    late = tick == ticks - 1 and left < 2
    behind = (tick or number) and not (late and left == 0)
    def chunk_of(tick):
        return (tick >= stage) & (tick - stage < CHUNKS), jnp.clip(tick - stage, 0, CHUNKS - 1)

    def entry(number, chunk):
        kind = jnp.where(core == number // layers, 0, 1)
        return (number % layers * CORES + kind) * CHUNKS + chunk

    valid, chunk = chunk_of(tick)
    place = entry(number, chunk)
    block_saves = [
        pltpu.make_async_copy(full_ref.at[b], saved_ref.at[place, b], save_sems.at[b])
        for b in range(blocks)
    ]
    if behind:
        before = (number - 1) % (CORES * layers)
        before_valid, before_chunk = chunk_of(tick - (number == 0))
        before_save = pltpu.make_async_copy(
            refs[0].at[0], saved_ref.at[entry(before, before_chunk), blocks], save_sems.at[blocks]
        )

    @pl.when(valid)
    def _():
        for copy in block_saves:
            copy.start()

    if behind:

        @pl.when(before_valid)
        def _():
            before_save.start()

    total = jnp.zeros((wide, rows), jnp.float32)
    for b in range(blocks):
        cosine = phase_ref[number, 0, b : b + 1, :]
        sine = phase_ref[number, 1, b : b + 1, :]
        real_part = full_ref[b, :split, :]
        imag_part = full_ref[b, split:, :]
        phased = jnp.concatenate(
            [cosine * real_part - sine * imag_part, sine * real_part + cosine * imag_part], axis=0
        ).astype(jnp.bfloat16)
        mat = mat_ref[:, b * rows : (b + 1) * rows]
        total += lax.dot_general(phased, mat, NT, preferred_element_type=jnp.float32)

    for b in range(blocks):
        out_ref[b] = total

    if late:
        sum_buf[...] = total
        sum_save = pltpu.make_async_copy(
            sum_buf, saved_ref.at[place, blocks], save_sems.at[blocks + 1]
        )

        @pl.when(valid)
        def _():
            sum_save.start()
            sum_save.wait()

    @pl.when(valid)
    def _():
        for copy in block_saves:
            copy.wait()

    if behind:

        @pl.when(before_valid)
        def _():
            before_save.wait()


def allocate_kernel(out_ref):
    pass


def allocate(shape):
    return pl.pallas_call(
        allocate_kernel,
        out_shape=jax.ShapeDtypeStruct(shape, jnp.float32),
        in_specs=[],
        out_specs=ANYWHERE,
        compiler_params=PARAMS,
    )()


def layer_step(full, phases, mat, saved, extra, **position):
    blocks, wide, rows = full.shape
    return pl.pallas_call(
        functools.partial(step_kernel, **position),
        out_shape=(
            jax.ShapeDtypeStruct(full.shape, jnp.float32),
            jax.ShapeDtypeStruct(saved.shape, jnp.float32),
        ),
        in_specs=[VMEM] * 3 + [ANYWHERE] * (1 + len(extra)),
        out_specs=(VMEM, ANYWHERE),
        input_output_aliases={3: 1},
        scratch_shapes=[
            pltpu.VMEM((wide, rows), jnp.float32),
            pltpu.SemaphoreType.DMA((blocks + 2,)),
        ],
        compiler_params=STEP_PARAMS,
        cost_estimate=pl.CostEstimate(
            flops=2 * wide * rows * rows * blocks,
            bytes_accessed=2 * blocks * rows * rows,
            transcendentals=0,
        ),
    )(full, phases, mat, saved, *extra)


def fields_kernel(
    core_ref, own_ref, other_ref, own_leave_ref, other_leave_ref, cos_ref, sin_ref, mat_ref, *refs
):
    out_ref, leave_ref, token_ref, total = refs[-4:]
    step = pl.program_id(0)
    chunks, gathered, wide, rows = other_ref.shape
    half = wide // 2
    first = core_ref[0] == 0

    def columns(mine_ref, theirs_ref, b, part):
        mine = mine_ref[:, b, part, :].reshape(chunks * half, rows)
        theirs = theirs_ref[:, b, part, :].reshape(chunks * half, rows)
        low = jnp.where(first, mine, theirs)
        high = jnp.where(first, theirs, mine)
        return jnp.concatenate([low, high], axis=0)

    spans = []
    for b in range(gathered):
        real_part = columns(own_ref, other_ref, b, slice(0, half))
        imag_part = columns(own_ref, other_ref, b, slice(half, wide))
        parts = [real_part.astype(jnp.bfloat16), imag_part.astype(jnp.bfloat16)]
        for depth in range(DEPTHS - 1):
            cosine = cos_ref[b, depth : depth + 1, :]
            sine = sin_ref[b, depth : depth + 1, :]
            parts.append((cosine * real_part - sine * imag_part).astype(jnp.bfloat16))
            parts.append((sine * real_part + cosine * imag_part).astype(jnp.bfloat16))
        spans.append(jnp.concatenate(parts, axis=0))
    depths = jnp.concatenate(spans, axis=1)
    partial = lax.dot_general(mat_ref[0], depths, NT, preferred_element_type=jnp.float32)

    @pl.when(step == 0)
    def _():
        total[...] = partial
        token_ref[...] = jnp.zeros_like(token_ref)
        leave = [
            columns(own_leave_ref, other_leave_ref, 0, part)
            for part in (slice(0, half), slice(half, wide))
        ]
        leave_ref[0] = jnp.concatenate(leave, axis=0).T

    @pl.when((step > 0) & (step < pl.num_programs(0) - 1))
    def _():
        total[...] += partial

    @pl.when(step == pl.num_programs(0) - 1)
    def _():
        out_ref[0] = (total[...] + partial).astype(jnp.bfloat16)


def layer_fields(core, own, other, cosines, sines, eigvec, layer, before):
    chunks, blocks, wide, rows = other.shape
    layers, _, orders = eigvec.shape
    blocks -= 1
    width = CORES * chunks * wide
    cols = DEPTHS * width
    entering = pl.BlockSpec((chunks, GATHERED, wide, rows), lambda b, c: (0, b, 0, 0))
    leave = pl.BlockSpec((chunks, 1, wide, rows), lambda b, c: (0, blocks, 0, 0))
    own_entering = pl.BlockSpec(
        (chunks, GATHERED, wide, rows), lambda b, c: (layer * CORES, b, 0, 0)
    )
    own_leave = pl.BlockSpec((chunks, 1, wide, rows), lambda b, c: (layer * CORES, blocks, 0, 0))
    coef = pl.BlockSpec((GATHERED, DEPTHS, rows), lambda b, c: (b, 0, 0))
    return pl.pallas_call(
        fields_kernel,
        out_shape=(
            jax.ShapeDtypeStruct((layers, rows, cols), jnp.bfloat16),
            jax.ShapeDtypeStruct((layers, rows, width), jnp.float32),
            jax.ShapeDtypeStruct((8, 128), jnp.float32),
        ),
        grid_spec=pltpu.PrefetchScalarGridSpec(
            num_scalar_prefetch=1,
            grid=(blocks // GATHERED,),
            in_specs=[
                own_entering,
                entering,
                own_leave,
                leave,
                coef,
                coef,
                pl.BlockSpec((1, rows, rows * GATHERED), lambda b, c: (layer, 0, b)),
            ]
            + [ANYWHERE] * len(before),
            out_specs=(
                pl.BlockSpec((1, rows, cols), lambda b, c: (layer, 0, 0)),
                pl.BlockSpec((1, rows, width), lambda b, c: (layer, 0, 0)),
                pl.BlockSpec((8, 128), lambda b, c: (0, 0)),
            ),
            scratch_shapes=[pltpu.VMEM((rows, cols), jnp.float32)],
        ),
        input_output_aliases={8: 0, 9: 1} if before else {},
        compiler_params=PARAMS,
    )(core, own, other, own, other, cosines, sines, eigvec, *before)


def to_all(block):
    return lax.all_to_all(block, "tile", split_axis=0, concat_axis=0, tiled=False)


def on_device(incident, interface, eigvec, angle, decay):
    groups = lax.axis_size("layer")
    tiles = lax.axis_size("tile")
    member = lax.axis_index("layer")
    core = (member % CORES).astype(jnp.int32)
    stage = (member // CORES).astype(jnp.int32)
    stages = groups // CORES
    layers, rows, orders = interface.shape
    width = incident.shape[1]
    part = width // 2 // CORES // CHUNKS
    wide = 2 * part
    partner = [(i, i ^ 1) for i in range(groups)]
    ring = [(i, (i + CORES) % groups) for i in range(groups)]

    phases = jnp.stack([angle, decay]).reshape(2, layers, tiles, rows)
    other_phases = lax.ppermute(phases, "layer", partner)
    def swap(layer, after):
        pieces = []
        for piece in range(PARTS):
            after = (widen(interface, layer, piece, after),)
            pieces.append(lax.ppermute(after[0], "layer", partner))
        return pieces, after

    arrived = [swap(0, ())[0]]
    mats = {}
    early = jnp.where(core == 0, phases, other_phases)
    late = jnp.where(core == 0, other_phases, phases)
    all_phases = jnp.concatenate([early, late], axis=1)
    scale = jnp.exp(-all_phases[1])
    whole = jnp.stack([scale * jnp.cos(all_phases[0]), scale * jnp.sin(all_phases[0])], axis=1)
    fracs = (jnp.arange(1, DEPTHS + 1, dtype=jnp.float32) / DEPTHS).reshape(1, 1, DEPTHS, 1)
    scale = jnp.exp(-fracs * phases[1][:, :, None, :])
    cosines = scale * jnp.cos(fracs * phases[0][:, :, None, :])
    sines = scale * jnp.sin(fracs * phases[0][:, :, None, :])

    whole, cosines, sines = lax.optimization_barrier((whole, cosines, sines))

    start = incident.astype(jnp.float32).T.reshape(2, CORES, CHUNKS, part, rows)
    start = jnp.where(core == 0, start[:, 0], start[:, 1])
    start = start.transpose(1, 0, 2, 3).reshape(CHUNKS, wide, rows)

    ticks = stages + CHUNKS - 1
    saved = allocate((SLOTS, tiles + 1, wide, rows))
    results = ()

    def finish(layer):
        first = (layer * CORES + 1) * CHUNKS
        other = lax.ppermute(saved[first : first + CHUNKS], "layer", partner)
        return layer_fields(
            core.reshape(1), saved, other, cosines[layer], sines[layer], eigvec, layer, results[:2]
        )

    received = None
    computed = ()
    for tick in range(ticks):
        inbox = start[min(tick, CHUNKS - 1)]
        if tick > 0:
            inbox = jnp.where(stage == 0, inbox, received)
        spread = jnp.broadcast_to(inbox[None], (tiles, wide, rows))
        for number in range(CORES * layers):
            full = to_all(spread)
            if tick == 0 and number < layers:
                pair = ()
                for piece in range(PARTS):
                    if number == 0 and piece == 0:
                        arrived += [swap(layer, (whole,))[0] for layer in range(1, layers)]
                    tied = pair + (spread,) * min(number, 1)
                    pair = tuple(place(interface, arrived[number][piece], number, piece, tied))
                for half in range(CORES):
                    mats[half * layers + number] = pair[half]
            if tick == ticks - 1 and number == CORES * layers - 1:
                results = finish(0)
                computed += tuple(results[2:])
            spread, saved = layer_step(
                full, whole, mats[number], saved, computed,
                tick=tick, number=number, layers=layers, ticks=ticks,
            )
            computed = (spread,)
        received = lax.ppermute(spread[0], "layer", ring)

    for layer in range(1, layers):
        results = finish(layer)
    return results[:2]


def solution(mesh):
    in_specs = (
        P("tile", None),
        P("layer", "tile", None),
        P("layer", "tile", None),
        P("layer", None),
        P("layer", None),
    )
    out_specs = (P("layer", "tile", None), P("layer", "tile", None))
    return jax.shard_map(
        on_device, mesh=mesh, in_specs=in_specs, out_specs=out_specs, check_vma=False
    )
```

```python
import functools

import jax
import jax.numpy as jnp
from jax import lax
from jax.experimental import pallas as pl
from jax.experimental.pallas import tpu as pltpu
from jax.sharding import PartitionSpec as P

DEPTHS = 4
CHUNKS = 2
CORES = 2
PARTS = 2
PIECES = 2
GATHERED = 4
NT = (((1,), (1,)), ((), ()))
VMEM = pl.BlockSpec(memory_space=pltpu.VMEM)
SMEM = pl.BlockSpec(memory_space=pltpu.SMEM)
ANYWHERE = pl.BlockSpec(memory_space=pl.ANY)
PLACE_PARAMS = pltpu.CompilerParams(vmem_limit_bytes=58 * 1024 * 1024)
STEP_PARAMS = pltpu.CompilerParams(vmem_limit_bytes=36 * 1024 * 1024)
PARAMS = pltpu.CompilerParams(vmem_limit_bytes=48 * 1024 * 1024)


def widen_kernel(mat_ref, *refs):
    refs[-1][...] = mat_ref[0].astype(jnp.float32)


def widen(mats, layer, part, after):
    rows, orders = mats.shape[1:]
    height = rows // PARTS
    piece = height // PIECES
    return pl.pallas_call(
        widen_kernel,
        out_shape=jax.ShapeDtypeStruct((height, orders), jnp.float32),
        grid=(PIECES,),
        in_specs=[
            pl.BlockSpec((1, piece, orders), lambda p: (layer, part * PIECES + p, 0)),
        ]
        + [ANYWHERE] * len(after),
        out_specs=pl.BlockSpec((piece, orders), lambda p: (p, 0)),
        compiler_params=PARAMS,
    )(mats, *after)


def place_kernel(own_ref, other_ref, *refs):
    early_ref, late_ref = refs[-2:]
    core = lax.rem(lax.axis_index("layer"), CORES)
    own = own_ref[0]
    other = other_ref[...].astype(jnp.bfloat16)

    @pl.when(core == 0)
    def _():
        early_ref[...] = own
        late_ref[...] = other

    @pl.when(core != 0)
    def _():
        early_ref[...] = other
        late_ref[...] = own


def place(mats, other, layer, part, before):
    height, orders = other.shape
    piece = height // PIECES
    out = jax.ShapeDtypeStruct((height * PARTS, orders), jnp.bfloat16)
    spec = pl.BlockSpec((piece, orders), lambda p: (part * PIECES + p, 0))
    return pl.pallas_call(
        place_kernel,
        out_shape=(out, out),
        grid=(PIECES,),
        in_specs=[
            pl.BlockSpec((1, piece, orders), lambda p: (layer, part * PIECES + p, 0)),
            pl.BlockSpec((piece, orders), lambda p: (p, 0)),
        ]
        + [ANYWHERE] * len(before),
        out_specs=(spec, spec),
        input_output_aliases={2: 0, 3: 1} if part > 0 else {},
        compiler_params=PLACE_PARAMS,
    )(mats, other, *before)


def step_kernel(full_ref, phase_ref, mat_ref, saved_in, out_ref, saved_ref, *, tick, number, layers):
    blocks, wide, rows = full_ref.shape
    split = wide // 2
    member = lax.axis_index("layer")
    core = lax.rem(member, CORES)
    chunk = tick - lax.div(member, CORES)
    total = jnp.zeros((wide, rows), jnp.float32)
    for b in range(blocks):
        cosine = phase_ref[number, 0, b : b + 1, :]
        sine = phase_ref[number, 1, b : b + 1, :]
        real_part = full_ref[b, :split, :]
        imag_part = full_ref[b, split:, :]
        phased = jnp.concatenate(
            [cosine * real_part - sine * imag_part, sine * real_part + cosine * imag_part], axis=0
        ).astype(jnp.bfloat16)
        mat = mat_ref[:, b * rows : (b + 1) * rows]
        total += lax.dot_general(phased, mat, NT, preferred_element_type=jnp.float32)

    for b in range(blocks):
        out_ref[b] = total

    for kind in range(CORES):
        for number_chunk in range(CHUNKS):

            @pl.when((chunk == number_chunk) & ((core != number // layers) == bool(kind)))
            def _():
                place = kind * CHUNKS + number_chunk
                for b in range(blocks):
                    saved_ref[place, b] = full_ref[b]
                saved_ref[place, blocks] = total


def allocate_kernel(out_ref):
    pass


def allocate(shape):
    return pl.pallas_call(
        allocate_kernel,
        out_shape=jax.ShapeDtypeStruct(shape, jnp.float32),
        in_specs=[],
        out_specs=VMEM,
        compiler_params=STEP_PARAMS,
    )()


def layer_step(full, phases, mat, saved, **position):
    blocks, wide, rows = full.shape
    return pl.pallas_call(
        functools.partial(step_kernel, **position),
        out_shape=(
            jax.ShapeDtypeStruct(full.shape, jnp.float32),
            jax.ShapeDtypeStruct(saved.shape, jnp.float32),
        ),
        in_specs=[VMEM] * 4,
        out_specs=(VMEM, VMEM),
        input_output_aliases={3: 1},
        compiler_params=STEP_PARAMS,
        cost_estimate=pl.CostEstimate(
            flops=2 * wide * rows * rows * blocks,
            bytes_accessed=2 * blocks * rows * rows,
            transcendentals=0,
        ),
    )(full, phases, mat, saved)


def fields_kernel(
    core_ref, own_ref, other_ref, own_leave_ref, other_leave_ref, cos_ref, sin_ref, mat_ref, *refs
):
    out_ref, leave_ref, total = refs[-3:]
    step = pl.program_id(0)
    chunks, gathered, wide, rows = other_ref.shape
    half = wide // 2
    first = core_ref[0] == 0

    def columns(mine_ref, theirs_ref, b, part):
        mine = mine_ref[:, b, part, :].reshape(chunks * half, rows)
        theirs = theirs_ref[:, b, part, :].reshape(chunks * half, rows)
        low = jnp.where(first, mine, theirs)
        high = jnp.where(first, theirs, mine)
        return jnp.concatenate([low, high], axis=0)

    spans = []
    for b in range(gathered):
        real_part = columns(own_ref, other_ref, b, slice(0, half))
        imag_part = columns(own_ref, other_ref, b, slice(half, wide))
        parts = [real_part.astype(jnp.bfloat16), imag_part.astype(jnp.bfloat16)]
        for depth in range(DEPTHS - 1):
            cosine = cos_ref[b, depth : depth + 1, :]
            sine = sin_ref[b, depth : depth + 1, :]
            parts.append((cosine * real_part - sine * imag_part).astype(jnp.bfloat16))
            parts.append((sine * real_part + cosine * imag_part).astype(jnp.bfloat16))
        spans.append(jnp.concatenate(parts, axis=0))
    depths = jnp.concatenate(spans, axis=1)
    partial = lax.dot_general(mat_ref[0], depths, NT, preferred_element_type=jnp.float32)

    @pl.when(step == 0)
    def _():
        total[...] = partial
        leave = [
            columns(own_leave_ref, other_leave_ref, 0, part)
            for part in (slice(0, half), slice(half, wide))
        ]
        leave_ref[0] = jnp.concatenate(leave, axis=0).T

    @pl.when((step > 0) & (step < pl.num_programs(0) - 1))
    def _():
        total[...] += partial

    @pl.when(step == pl.num_programs(0) - 1)
    def _():
        out_ref[0] = (total[...] + partial).astype(jnp.bfloat16)


def layer_fields(core, own, other, cosines, sines, eigvec, layer, before):
    chunks, blocks, wide, rows = other.shape
    layers, _, orders = eigvec.shape
    blocks -= 1
    width = CORES * chunks * wide
    cols = DEPTHS * width
    entering = pl.BlockSpec((chunks, GATHERED, wide, rows), lambda b, c: (0, b, 0, 0))
    leave = pl.BlockSpec((chunks, 1, wide, rows), lambda b, c: (0, blocks, 0, 0))
    own_entering = pl.BlockSpec(
        (chunks, GATHERED, wide, rows), lambda b, c: (0, b, 0, 0)
    )
    own_leave = pl.BlockSpec((chunks, 1, wide, rows), lambda b, c: (0, blocks, 0, 0))
    coef = pl.BlockSpec((GATHERED, DEPTHS, rows), lambda b, c: (b, 0, 0))
    return pl.pallas_call(
        fields_kernel,
        out_shape=(
            jax.ShapeDtypeStruct((layers, rows, cols), jnp.bfloat16),
            jax.ShapeDtypeStruct((layers, rows, width), jnp.float32),
        ),
        grid_spec=pltpu.PrefetchScalarGridSpec(
            num_scalar_prefetch=1,
            grid=(blocks // GATHERED,),
            in_specs=[
                own_entering,
                entering,
                own_leave,
                leave,
                coef,
                coef,
                pl.BlockSpec((1, rows, rows * GATHERED), lambda b, c: (layer, 0, b)),
            ]
            + [ANYWHERE] * len(before),
            out_specs=(
                pl.BlockSpec((1, rows, cols), lambda b, c: (layer, 0, 0)),
                pl.BlockSpec((1, rows, width), lambda b, c: (layer, 0, 0)),
            ),
            scratch_shapes=[pltpu.VMEM((rows, cols), jnp.float32)],
        ),
        input_output_aliases={8: 0, 9: 1} if before else {},
        compiler_params=PARAMS,
    )(core, own, other, own, other, cosines, sines, eigvec, *before)


def to_all(block):
    return lax.all_to_all(block, "tile", split_axis=0, concat_axis=0, tiled=False)


def on_device(incident, interface, eigvec, angle, decay):
    groups = lax.axis_size("layer")
    tiles = lax.axis_size("tile")
    member = lax.axis_index("layer")
    core = (member % CORES).astype(jnp.int32)
    stage = (member // CORES).astype(jnp.int32)
    stages = groups // CORES
    layers, rows, orders = interface.shape
    width = incident.shape[1]
    part = width // 2 // CORES // CHUNKS
    wide = 2 * part
    partner = [(i, i ^ 1) for i in range(groups)]
    ring = [(i, (i + CORES) % groups) for i in range(groups)]

    phases = jnp.stack([angle, decay]).reshape(2, layers, tiles, rows)
    other_phases = lax.ppermute(phases, "layer", partner)
    def swap(layer, after):
        pieces = []
        for piece in range(PARTS):
            after = (widen(interface, layer, piece, after),)
            pieces.append(lax.ppermute(after[0], "layer", partner))
        return pieces, after

    arrived = [swap(0, ())[0]]
    mats = {}
    early = jnp.where(core == 0, phases, other_phases)
    late = jnp.where(core == 0, other_phases, phases)
    all_phases = jnp.concatenate([early, late], axis=1)
    scale = jnp.exp(-all_phases[1])
    whole = jnp.stack([scale * jnp.cos(all_phases[0]), scale * jnp.sin(all_phases[0])], axis=1)
    fracs = (jnp.arange(1, DEPTHS + 1, dtype=jnp.float32) / DEPTHS).reshape(1, 1, DEPTHS, 1)
    scale = jnp.exp(-fracs * phases[1][:, :, None, :])
    cosines = scale * jnp.cos(fracs * phases[0][:, :, None, :])
    sines = scale * jnp.sin(fracs * phases[0][:, :, None, :])

    whole, cosines, sines = lax.optimization_barrier((whole, cosines, sines))

    start = incident.astype(jnp.float32).T.reshape(2, CORES, CHUNKS, part, rows)
    start = jnp.where(core == 0, start[:, 0], start[:, 1])
    start = start.transpose(1, 0, 2, 3).reshape(CHUNKS, wide, rows)

    ticks = stages + CHUNKS - 1
    saved = [allocate((CORES * CHUNKS, tiles + 1, wide, rows)) for _ in range(layers)]
    results = ()

    def finish(layer):
        other = lax.ppermute(saved[layer][CHUNKS:], "layer", partner)
        return layer_fields(
            core.reshape(1), saved[layer], other, cosines[layer], sines[layer], eigvec, layer, results
        )

    received = None
    for tick in range(ticks):
        inbox = start[min(tick, CHUNKS - 1)]
        if tick > 0:
            inbox = jnp.where(stage == 0, inbox, received)
        spread = jnp.broadcast_to(inbox[None], (tiles, wide, rows))
        for number in range(CORES * layers):
            full = to_all(spread)
            if tick == 0 and number < layers:
                pair = ()
                for piece in range(PARTS):
                    if number == 0 and piece == 0:
                        arrived += [swap(layer, (whole,))[0] for layer in range(1, layers)]
                    tied = pair + (spread,) * min(number, 1)
                    pair = tuple(place(interface, arrived[number][piece], number, piece, tied))
                for half in range(CORES):
                    mats[half * layers + number] = pair[half]
            own = number % layers
            spread, saved[own] = layer_step(
                full, whole, mats[number], saved[own], tick=tick, number=number, layers=layers
            )
        received = lax.ppermute(spread[0], "layer", ring)

    for layer in range(layers):
        results = finish(layer)
    return results


def solution(mesh):
    in_specs = (
        P("tile", None),
        P("layer", "tile", None),
        P("layer", "tile", None),
        P("layer", None),
        P("layer", None),
    )
    out_specs = (P("layer", "tile", None), P("layer", "tile", None))
    return jax.shard_map(
        on_device, mesh=mesh, in_specs=in_specs, out_specs=out_specs, check_vma=False
    )
```

```python
import functools

import jax
import jax.numpy as jnp
from jax import lax
from jax.experimental import pallas as pl
from jax.experimental.pallas import tpu as pltpu
from jax.sharding import PartitionSpec as P

DEPTHS = 4
CHUNKS = 2
CORES = 2
PARTS = 2
PIECES = 2
GATHERED = 4
NT = (((1,), (1,)), ((), ()))
VMEM = pl.BlockSpec(memory_space=pltpu.VMEM)
SMEM = pl.BlockSpec(memory_space=pltpu.SMEM)
ANYWHERE = pl.BlockSpec(memory_space=pl.ANY)
PLACE_PARAMS = pltpu.CompilerParams(vmem_limit_bytes=58 * 1024 * 1024)
STEP_PARAMS = pltpu.CompilerParams(vmem_limit_bytes=12 * 1024 * 1024)
PARAMS = pltpu.CompilerParams(vmem_limit_bytes=48 * 1024 * 1024)


def widen_kernel(mat_ref, *refs):
    refs[-1][...] = mat_ref[0].astype(jnp.float32)


def widen(mats, layer, part, after):
    rows, orders = mats.shape[1:]
    height = rows // PARTS
    piece = height // PIECES
    return pl.pallas_call(
        widen_kernel,
        out_shape=jax.ShapeDtypeStruct((height, orders), jnp.float32),
        grid=(PIECES,),
        in_specs=[
            pl.BlockSpec((1, piece, orders), lambda p: (layer, part * PIECES + p, 0)),
        ]
        + [ANYWHERE] * len(after),
        out_specs=pl.BlockSpec((piece, orders), lambda p: (p, 0)),
        compiler_params=PARAMS,
    )(mats, *after)


def place_kernel(own_ref, other_ref, *refs):
    early_ref, late_ref = refs[-2:]
    core = lax.rem(lax.axis_index("layer"), CORES)
    own = own_ref[0]
    other = other_ref[...].astype(jnp.bfloat16)

    @pl.when(core == 0)
    def _():
        early_ref[...] = own
        late_ref[...] = other

    @pl.when(core != 0)
    def _():
        early_ref[...] = other
        late_ref[...] = own


def place(mats, other, layer, part, before):
    height, orders = other.shape
    piece = height // PIECES
    out = jax.ShapeDtypeStruct((height * PARTS, orders), jnp.bfloat16)
    spec = pl.BlockSpec((piece, orders), lambda p: (part * PIECES + p, 0))
    return pl.pallas_call(
        place_kernel,
        out_shape=(out, out),
        grid=(PIECES,),
        in_specs=[
            pl.BlockSpec((1, piece, orders), lambda p: (layer, part * PIECES + p, 0)),
            pl.BlockSpec((piece, orders), lambda p: (p, 0)),
        ]
        + [ANYWHERE] * len(before),
        out_specs=(spec, spec),
        input_output_aliases={2: 0, 3: 1} if part > 0 else {},
        compiler_params=PLACE_PARAMS,
    )(mats, other, *before)


def step_kernel(full_ref, phase_ref, mat_ref, saved_in, out_ref, saved_ref, *, tick, number, layers):
    blocks, wide, rows = full_ref.shape
    split = wide // 2
    member = lax.axis_index("layer")
    core = lax.rem(member, CORES)
    chunk = tick - lax.div(member, CORES)
    total = jnp.zeros((wide, rows), jnp.float32)
    for b in range(blocks):
        cosine = phase_ref[number, 0, b : b + 1, :]
        sine = phase_ref[number, 1, b : b + 1, :]
        real_part = full_ref[b, :split, :]
        imag_part = full_ref[b, split:, :]
        phased = jnp.concatenate(
            [cosine * real_part - sine * imag_part, sine * real_part + cosine * imag_part], axis=0
        ).astype(jnp.bfloat16)
        mat = mat_ref[:, b * rows : (b + 1) * rows]
        total += lax.dot_general(phased, mat, NT, preferred_element_type=jnp.float32)

    for b in range(blocks):
        out_ref[b] = total

    for kind in range(CORES):
        for number_chunk in range(CHUNKS):

            @pl.when((chunk == number_chunk) & ((core != number // layers) == bool(kind)))
            def _():
                place = kind * CHUNKS + number_chunk
                for b in range(blocks):
                    saved_ref[place, b] = full_ref[b]
                saved_ref[place, blocks] = total


def allocate_kernel(after_ref, out_ref):
    pass


def allocate(shape, after):
    return pl.pallas_call(
        allocate_kernel,
        out_shape=jax.ShapeDtypeStruct(shape, jnp.float32),
        in_specs=[ANYWHERE],
        out_specs=VMEM,
        compiler_params=STEP_PARAMS,
    )(after)


def layer_step(full, phases, mat, saved, **position):
    blocks, wide, rows = full.shape
    return pl.pallas_call(
        functools.partial(step_kernel, **position),
        out_shape=(
            jax.ShapeDtypeStruct(full.shape, jnp.float32),
            jax.ShapeDtypeStruct(saved.shape, jnp.float32),
        ),
        in_specs=[VMEM] * 4,
        out_specs=(VMEM, VMEM),
        input_output_aliases={3: 1},
        compiler_params=STEP_PARAMS,
        cost_estimate=pl.CostEstimate(
            flops=2 * wide * rows * rows * blocks,
            bytes_accessed=2 * blocks * rows * rows,
            transcendentals=0,
        ),
    )(full, phases, mat, saved)


def fields_kernel(
    core_ref, own_ref, other_ref, own_leave_ref, other_leave_ref, cos_ref, sin_ref, mat_ref, *refs
):
    out_ref, leave_ref, total = refs[-3:]
    step = pl.program_id(0)
    chunks, gathered, wide, rows = other_ref.shape
    half = wide // 2
    first = core_ref[0] == 0

    def columns(mine_ref, theirs_ref, b, part):
        mine = mine_ref[:, b, part, :].reshape(chunks * half, rows)
        theirs = theirs_ref[:, b, part, :].reshape(chunks * half, rows)
        low = jnp.where(first, mine, theirs)
        high = jnp.where(first, theirs, mine)
        return jnp.concatenate([low, high], axis=0)

    spans = []
    for b in range(gathered):
        real_part = columns(own_ref, other_ref, b, slice(0, half))
        imag_part = columns(own_ref, other_ref, b, slice(half, wide))
        parts = [real_part.astype(jnp.bfloat16), imag_part.astype(jnp.bfloat16)]
        for depth in range(DEPTHS - 1):
            cosine = cos_ref[b, depth : depth + 1, :]
            sine = sin_ref[b, depth : depth + 1, :]
            parts.append((cosine * real_part - sine * imag_part).astype(jnp.bfloat16))
            parts.append((sine * real_part + cosine * imag_part).astype(jnp.bfloat16))
        spans.append(jnp.concatenate(parts, axis=0))
    depths = jnp.concatenate(spans, axis=1)
    partial = lax.dot_general(mat_ref[0], depths, NT, preferred_element_type=jnp.float32)

    @pl.when(step == 0)
    def _():
        total[...] = partial
        leave = [
            columns(own_leave_ref, other_leave_ref, 0, part)
            for part in (slice(0, half), slice(half, wide))
        ]
        leave_ref[0] = jnp.concatenate(leave, axis=0).T

    @pl.when((step > 0) & (step < pl.num_programs(0) - 1))
    def _():
        total[...] += partial

    @pl.when(step == pl.num_programs(0) - 1)
    def _():
        out_ref[0] = (total[...] + partial).astype(jnp.bfloat16)


def layer_fields(core, own, other, cosines, sines, eigvec, layer, before):
    chunks, blocks, wide, rows = other.shape
    layers, _, orders = eigvec.shape
    blocks -= 1
    width = CORES * chunks * wide
    cols = DEPTHS * width
    entering = pl.BlockSpec((chunks, GATHERED, wide, rows), lambda b, c: (0, b, 0, 0))
    leave = pl.BlockSpec((chunks, 1, wide, rows), lambda b, c: (0, blocks, 0, 0))
    own_entering = pl.BlockSpec(
        (chunks, GATHERED, wide, rows), lambda b, c: (0, b, 0, 0)
    )
    own_leave = pl.BlockSpec((chunks, 1, wide, rows), lambda b, c: (0, blocks, 0, 0))
    coef = pl.BlockSpec((GATHERED, DEPTHS, rows), lambda b, c: (b, 0, 0))
    return pl.pallas_call(
        fields_kernel,
        out_shape=(
            jax.ShapeDtypeStruct((layers, rows, cols), jnp.bfloat16),
            jax.ShapeDtypeStruct((layers, rows, width), jnp.float32),
        ),
        grid_spec=pltpu.PrefetchScalarGridSpec(
            num_scalar_prefetch=1,
            grid=(blocks // GATHERED,),
            in_specs=[
                own_entering,
                entering,
                own_leave,
                leave,
                coef,
                coef,
                pl.BlockSpec((1, rows, rows * GATHERED), lambda b, c: (layer, 0, b)),
            ]
            + [ANYWHERE] * len(before),
            out_specs=(
                pl.BlockSpec((1, rows, cols), lambda b, c: (layer, 0, 0)),
                pl.BlockSpec((1, rows, width), lambda b, c: (layer, 0, 0)),
            ),
            scratch_shapes=[pltpu.VMEM((rows, cols), jnp.float32)],
        ),
        input_output_aliases={8: 0, 9: 1} if before else {},
        compiler_params=PARAMS,
    )(core, own, other, own, other, cosines, sines, eigvec, *before)


def to_all(block):
    return lax.all_to_all(block, "tile", split_axis=0, concat_axis=0, tiled=False)


def on_device(incident, interface, eigvec, angle, decay):
    groups = lax.axis_size("layer")
    tiles = lax.axis_size("tile")
    member = lax.axis_index("layer")
    core = (member % CORES).astype(jnp.int32)
    stage = (member // CORES).astype(jnp.int32)
    stages = groups // CORES
    layers, rows, orders = interface.shape
    width = incident.shape[1]
    part = width // 2 // CORES // CHUNKS
    wide = 2 * part
    partner = [(i, i ^ 1) for i in range(groups)]
    ring = [(i, (i + CORES) % groups) for i in range(groups)]

    phases = jnp.stack([angle, decay]).reshape(2, layers, tiles, rows)
    other_phases = lax.ppermute(phases, "layer", partner)
    def swap(layer, after):
        pieces = []
        for piece in range(PARTS):
            after = (widen(interface, layer, piece, after),)
            pieces.append(lax.ppermute(after[0], "layer", partner))
        return pieces, after

    arrived = [swap(0, ())[0]]
    mats = {}
    early = jnp.where(core == 0, phases, other_phases)
    late = jnp.where(core == 0, other_phases, phases)
    all_phases = jnp.concatenate([early, late], axis=1)
    scale = jnp.exp(-all_phases[1])
    whole = jnp.stack([scale * jnp.cos(all_phases[0]), scale * jnp.sin(all_phases[0])], axis=1)
    fracs = (jnp.arange(1, DEPTHS + 1, dtype=jnp.float32) / DEPTHS).reshape(1, 1, DEPTHS, 1)
    scale = jnp.exp(-fracs * phases[1][:, :, None, :])
    cosines = scale * jnp.cos(fracs * phases[0][:, :, None, :])
    sines = scale * jnp.sin(fracs * phases[0][:, :, None, :])

    whole, cosines, sines = lax.optimization_barrier((whole, cosines, sines))

    start = incident.astype(jnp.float32).T.reshape(2, CORES, CHUNKS, part, rows)
    start = jnp.where(core == 0, start[:, 0], start[:, 1])
    start = start.transpose(1, 0, 2, 3).reshape(CHUNKS, wide, rows)

    ticks = stages + CHUNKS - 1
    saved = []
    results = ()

    def finish(layer):
        other = lax.ppermute(saved[layer][CHUNKS:], "layer", partner)
        return layer_fields(
            core.reshape(1), saved[layer], other, cosines[layer], sines[layer], eigvec, layer, results
        )

    received = None
    for tick in range(ticks):
        inbox = start[min(tick, CHUNKS - 1)]
        if tick > 0:
            inbox = jnp.where(stage == 0, inbox, received)
        spread = jnp.broadcast_to(inbox[None], (tiles, wide, rows))
        for number in range(CORES * layers):
            full = to_all(spread)
            if tick == 0 and number < layers:
                pair = ()
                for piece in range(PARTS):
                    if number == 0 and piece == 0:
                        arrived += [swap(layer, (whole,))[0] for layer in range(1, layers)]
                    tied = pair + (spread,) * min(number, 1)
                    pair = tuple(place(interface, arrived[number][piece], number, piece, tied))
                for half in range(CORES):
                    mats[half * layers + number] = pair[half]
            own = number % layers
            if tick == 0 and number < layers:
                after = full if number else spread
                saved.append(allocate((CORES * CHUNKS, tiles + 1, wide, rows), after))
            spread, saved[own] = layer_step(
                full, whole, mats[number], saved[own], tick=tick, number=number, layers=layers
            )
        received = lax.ppermute(spread[0], "layer", ring)

    saved = lax.optimization_barrier(saved)
    for layer in range(layers):
        results = finish(layer)
    return results


def solution(mesh):
    in_specs = (
        P("tile", None),
        P("layer", "tile", None),
        P("layer", "tile", None),
        P("layer", None),
        P("layer", None),
    )
    out_specs = (P("layer", "tile", None), P("layer", "tile", None))
    return jax.shard_map(
        on_device, mesh=mesh, in_specs=in_specs, out_specs=out_specs, check_vma=False
    )
```

```python
import functools

import jax
import jax.numpy as jnp
from jax import lax
from jax.experimental import pallas as pl
from jax.experimental.pallas import tpu as pltpu
from jax.sharding import PartitionSpec as P

DEPTHS = 4
CHUNKS = 2
CORES = 2
PARTS = 2
PIECES = 1
GATHERED = 4
NT = (((1,), (1,)), ((), ()))
VMEM = pl.BlockSpec(memory_space=pltpu.VMEM)
SMEM = pl.BlockSpec(memory_space=pltpu.SMEM)
ANYWHERE = pl.BlockSpec(memory_space=pl.ANY)
PLACE_PARAMS = pltpu.CompilerParams(vmem_limit_bytes=58 * 1024 * 1024)
STEP_PARAMS = pltpu.CompilerParams(vmem_limit_bytes=12 * 1024 * 1024)
PARAMS = pltpu.CompilerParams(vmem_limit_bytes=48 * 1024 * 1024)


def widen_kernel(mat_ref, *refs):
    refs[-1][...] = mat_ref[0].astype(jnp.float32)


def widen(mats, layer, part, after):
    rows, orders = mats.shape[1:]
    height = rows // PARTS
    piece = height // PIECES
    return pl.pallas_call(
        widen_kernel,
        out_shape=jax.ShapeDtypeStruct((height, orders), jnp.float32),
        grid=(PIECES,),
        in_specs=[
            pl.BlockSpec((1, piece, orders), lambda p: (layer, part * PIECES + p, 0)),
        ]
        + [ANYWHERE] * len(after),
        out_specs=pl.BlockSpec((piece, orders), lambda p: (p, 0)),
        compiler_params=PARAMS,
    )(mats, *after)


def place_kernel(own_ref, other_ref, *refs):
    early_ref, late_ref = refs[-2:]
    core = lax.rem(lax.axis_index("layer"), CORES)
    own = own_ref[0]
    other = other_ref[...].astype(jnp.bfloat16)

    @pl.when(core == 0)
    def _():
        early_ref[...] = own
        late_ref[...] = other

    @pl.when(core != 0)
    def _():
        early_ref[...] = other
        late_ref[...] = own


def place(mats, other, layer, part, before):
    height, orders = other.shape
    piece = height // PIECES
    out = jax.ShapeDtypeStruct((height * PARTS, orders), jnp.bfloat16)
    spec = pl.BlockSpec((piece, orders), lambda p: (part * PIECES + p, 0))
    return pl.pallas_call(
        place_kernel,
        out_shape=(out, out),
        grid=(PIECES,),
        in_specs=[
            pl.BlockSpec((1, piece, orders), lambda p: (layer, part * PIECES + p, 0)),
            pl.BlockSpec((piece, orders), lambda p: (p, 0)),
        ]
        + [ANYWHERE] * len(before),
        out_specs=(spec, spec),
        input_output_aliases={2: 0, 3: 1} if part > 0 else {},
        compiler_params=PLACE_PARAMS,
    )(mats, other, *before)


def step_kernel(full_ref, phase_ref, mat_ref, saved_in, out_ref, saved_ref, *, tick, number, layers):
    blocks, wide, rows = full_ref.shape
    split = wide // 2
    member = lax.axis_index("layer")
    core = lax.rem(member, CORES)
    chunk = tick - lax.div(member, CORES)
    total = jnp.zeros((wide, rows), jnp.float32)
    for b in range(blocks):
        cosine = phase_ref[number, 0, b : b + 1, :]
        sine = phase_ref[number, 1, b : b + 1, :]
        real_part = full_ref[b, :split, :]
        imag_part = full_ref[b, split:, :]
        phased = jnp.concatenate(
            [cosine * real_part - sine * imag_part, sine * real_part + cosine * imag_part], axis=0
        ).astype(jnp.bfloat16)
        mat = mat_ref[:, b * rows : (b + 1) * rows]
        total += lax.dot_general(phased, mat, NT, preferred_element_type=jnp.float32)

    for b in range(blocks):
        out_ref[b] = total

    for kind in range(CORES):
        for number_chunk in range(CHUNKS):

            @pl.when((chunk == number_chunk) & ((core != number // layers) == bool(kind)))
            def _():
                place = kind * CHUNKS + number_chunk
                for b in range(blocks):
                    saved_ref[place, b] = full_ref[b]
                saved_ref[place, blocks] = total


def allocate_kernel(after_ref, out_ref):
    pass


def allocate(shape, after):
    return pl.pallas_call(
        allocate_kernel,
        out_shape=jax.ShapeDtypeStruct(shape, jnp.float32),
        in_specs=[ANYWHERE],
        out_specs=VMEM,
        compiler_params=STEP_PARAMS,
    )(after)


def layer_step(full, phases, mat, saved, **position):
    blocks, wide, rows = full.shape
    return pl.pallas_call(
        functools.partial(step_kernel, **position),
        out_shape=(
            jax.ShapeDtypeStruct(full.shape, jnp.float32),
            jax.ShapeDtypeStruct(saved.shape, jnp.float32),
        ),
        in_specs=[VMEM] * 4,
        out_specs=(VMEM, VMEM),
        input_output_aliases={3: 1},
        compiler_params=STEP_PARAMS,
        cost_estimate=pl.CostEstimate(
            flops=2 * wide * rows * rows * blocks,
            bytes_accessed=2 * blocks * rows * rows,
            transcendentals=0,
        ),
    )(full, phases, mat, saved)


def fields_kernel(
    core_ref, own_ref, other_ref, own_leave_ref, other_leave_ref, cos_ref, sin_ref, mat_ref, *refs
):
    out_ref, leave_ref, total = refs[-3:]
    step = pl.program_id(0)
    chunks, gathered, wide, rows = other_ref.shape
    half = wide // 2
    first = core_ref[0] == 0

    def columns(mine_ref, theirs_ref, b, part):
        mine = mine_ref[:, b, part, :].reshape(chunks * half, rows)
        theirs = theirs_ref[:, b, part, :].reshape(chunks * half, rows)
        low = jnp.where(first, mine, theirs)
        high = jnp.where(first, theirs, mine)
        return jnp.concatenate([low, high], axis=0)

    spans = []
    for b in range(gathered):
        real_part = columns(own_ref, other_ref, b, slice(0, half))
        imag_part = columns(own_ref, other_ref, b, slice(half, wide))
        parts = [real_part.astype(jnp.bfloat16), imag_part.astype(jnp.bfloat16)]
        for depth in range(DEPTHS - 1):
            cosine = cos_ref[b, depth : depth + 1, :]
            sine = sin_ref[b, depth : depth + 1, :]
            parts.append((cosine * real_part - sine * imag_part).astype(jnp.bfloat16))
            parts.append((sine * real_part + cosine * imag_part).astype(jnp.bfloat16))
        spans.append(jnp.concatenate(parts, axis=0))
    depths = jnp.concatenate(spans, axis=1)
    partial = lax.dot_general(mat_ref[0], depths, NT, preferred_element_type=jnp.float32)

    @pl.when(step == 0)
    def _():
        total[...] = partial
        leave = [
            columns(own_leave_ref, other_leave_ref, 0, part)
            for part in (slice(0, half), slice(half, wide))
        ]
        leave_ref[0] = jnp.concatenate(leave, axis=0).T

    @pl.when((step > 0) & (step < pl.num_programs(0) - 1))
    def _():
        total[...] += partial

    @pl.when(step == pl.num_programs(0) - 1)
    def _():
        out_ref[0] = (total[...] + partial).astype(jnp.bfloat16)


def layer_fields(core, own, other, cosines, sines, eigvec, layer, before):
    chunks, blocks, wide, rows = other.shape
    layers, _, orders = eigvec.shape
    blocks -= 1
    width = CORES * chunks * wide
    cols = DEPTHS * width
    entering = pl.BlockSpec((chunks, GATHERED, wide, rows), lambda b, c: (0, b, 0, 0))
    leave = pl.BlockSpec((chunks, 1, wide, rows), lambda b, c: (0, blocks, 0, 0))
    own_entering = pl.BlockSpec(
        (chunks, GATHERED, wide, rows), lambda b, c: (0, b, 0, 0)
    )
    own_leave = pl.BlockSpec((chunks, 1, wide, rows), lambda b, c: (0, blocks, 0, 0))
    coef = pl.BlockSpec((GATHERED, DEPTHS, rows), lambda b, c: (b, 0, 0))
    return pl.pallas_call(
        fields_kernel,
        out_shape=(
            jax.ShapeDtypeStruct((layers, rows, cols), jnp.bfloat16),
            jax.ShapeDtypeStruct((layers, rows, width), jnp.float32),
        ),
        grid_spec=pltpu.PrefetchScalarGridSpec(
            num_scalar_prefetch=1,
            grid=(blocks // GATHERED,),
            in_specs=[
                own_entering,
                entering,
                own_leave,
                leave,
                coef,
                coef,
                pl.BlockSpec((1, rows, rows * GATHERED), lambda b, c: (layer, 0, b)),
            ]
            + [ANYWHERE] * len(before),
            out_specs=(
                pl.BlockSpec((1, rows, cols), lambda b, c: (layer, 0, 0)),
                pl.BlockSpec((1, rows, width), lambda b, c: (layer, 0, 0)),
            ),
            scratch_shapes=[pltpu.VMEM((rows, cols), jnp.float32)],
        ),
        input_output_aliases={8: 0, 9: 1} if before else {},
        compiler_params=PARAMS,
    )(core, own, other, own, other, cosines, sines, eigvec, *before)


def to_all(block):
    return lax.all_to_all(block, "tile", split_axis=0, concat_axis=0, tiled=False)


def on_device(incident, interface, eigvec, angle, decay):
    groups = lax.axis_size("layer")
    tiles = lax.axis_size("tile")
    member = lax.axis_index("layer")
    core = (member % CORES).astype(jnp.int32)
    stage = (member // CORES).astype(jnp.int32)
    stages = groups // CORES
    layers, rows, orders = interface.shape
    width = incident.shape[1]
    part = width // 2 // CORES // CHUNKS
    wide = 2 * part
    partner = [(i, i ^ 1) for i in range(groups)]
    ring = [(i, (i + CORES) % groups) for i in range(groups)]

    phases = jnp.stack([angle, decay]).reshape(2, layers, tiles, rows)
    other_phases = lax.ppermute(phases, "layer", partner)
    def swap(layer, after):
        pieces = []
        for piece in range(PARTS):
            after = (widen(interface, layer, piece, after),)
            pieces.append(lax.ppermute(after[0], "layer", partner))
        return pieces, after

    arrived = [swap(0, ())[0]]
    mats = {}
    early = jnp.where(core == 0, phases, other_phases)
    late = jnp.where(core == 0, other_phases, phases)
    all_phases = jnp.concatenate([early, late], axis=1)
    scale = jnp.exp(-all_phases[1])
    whole = jnp.stack([scale * jnp.cos(all_phases[0]), scale * jnp.sin(all_phases[0])], axis=1)
    fracs = (jnp.arange(1, DEPTHS + 1, dtype=jnp.float32) / DEPTHS).reshape(1, 1, DEPTHS, 1)

    start = incident.astype(jnp.float32).T.reshape(2, CORES, CHUNKS, part, rows)
    start = jnp.where(core == 0, start[:, 0], start[:, 1])
    start = start.transpose(1, 0, 2, 3).reshape(CHUNKS, wide, rows)

    ticks = stages + CHUNKS - 1
    saved = []
    results = ()

    def finish(layer):
        other = lax.ppermute(saved[layer][CHUNKS:], "layer", partner)
        return layer_fields(
            core.reshape(1), saved[layer], other, cosines[layer], sines[layer], eigvec, layer, results
        )

    received = None
    for tick in range(ticks):
        inbox = start[min(tick, CHUNKS - 1)]
        if tick > 0:
            inbox = jnp.where(stage == 0, inbox, received)
        spread = jnp.broadcast_to(inbox[None], (tiles, wide, rows))
        for number in range(CORES * layers):
            full = to_all(spread)
            if tick == 0 and number < layers:
                pair = ()
                for piece in range(PARTS):
                    if number == 0 and piece == 0:
                        arrived += [swap(layer, (whole,))[0] for layer in range(1, layers)]
                    tied = pair + (spread,) * min(number, 1)
                    pair = tuple(place(interface, arrived[number][piece], number, piece, tied))
                for half in range(CORES):
                    mats[half * layers + number] = pair[half]
            own = number % layers
            if tick == 0 and number == 1:
                scale = jnp.exp(-fracs * later_phases[1][:, :, None, :])
                cosines = scale * jnp.cos(fracs * later_phases[0][:, :, None, :])
                sines = scale * jnp.sin(fracs * later_phases[0][:, :, None, :])
                full, cosines, sines = lax.optimization_barrier((full, cosines, sines))
            if tick == 0 and number < layers:
                after = full if number else spread
                saved.append(allocate((CORES * CHUNKS, tiles + 1, wide, rows), after))
            spread, saved[own] = layer_step(
                full, whole, mats[number], saved[own], tick=tick, number=number, layers=layers
            )
            if tick == 0 and number == 0:
                spread, later_phases = lax.optimization_barrier((spread, phases))
        received = lax.ppermute(spread[0], "layer", ring)

    saved = lax.optimization_barrier(saved)
    for layer in range(layers):
        results = finish(layer)
    return results


def solution(mesh):
    in_specs = (
        P("tile", None),
        P("layer", "tile", None),
        P("layer", "tile", None),
        P("layer", None),
        P("layer", None),
    )
    out_specs = (P("layer", "tile", None), P("layer", "tile", None))
    return jax.shard_map(
        on_device, mesh=mesh, in_specs=in_specs, out_specs=out_specs, check_vma=False
    )
```
